32 devices in a mesh: dp: 8 (over z, x), tensor: 4 (over y, core).
Axes of the slice: x: 2, y: 2, z: 4, core: 2. Of those that a mesh axis runs over, the one named last changes fastest.
Arguments:
- hidden: bfloat16 [2048, 2, 8192], P('dp', None, 'tensor'), may hold values from -6 to 6
- key_value_weight: bfloat16 [8192, 2048], P('tensor'), may hold values from -0.0625 to 0.0625
- adapter_down_weight: bfloat16 [128, 8192, 64], P('dp', 'tensor'), may hold values from -0.0625 to 0.0625
- adapter_up_weight: bfloat16 [128, 64, 2048], P('dp', None, 'tensor'), may hold values from -0.75 to 0.75
- attempt_adapter_slot: int32 [2048, 1], P('dp'), may hold values from 0 to 7; in each aligned block of 256 rows (0 to 255, 256 to 511, ...) at most 128 rows name the same one
- group_slot_task: int32 [8, 8], replicated, may hold values from 0 to 127, as said below
- task_row_position: int32 [128], replicated, may hold values from 0 to 127, as said below
- scores: int32 [2048], P('dp'), may hold values 0 or 1
- cotangent: bfloat16 [2048, 2, 2048], P('dp', None, 'tensor'), may hold values from -6 to 6
Outputs:
- kv_new: bfloat16 [2048, 2, 2048], P('dp', None, 'tensor')
- grad_down: bfloat16 [128, 8192, 64], P('dp', 'tensor')
- grad_up: bfloat16 [128, 64, 2048], P('dp', None, 'tensor')
The draws below stay inside these ranges and needn't reach their ends.
Inputs may be any that keep to these rules, and one draw needn't show every extreme that they name: `attempt_adapter_slot`: among the 256 attempts of one group (aligned blocks of 256 rows), at most 128 name the same slot, and exactly 128 do in some block. `task_row_position`: every row is named once; rows o * 16 to (o + 1) * 16 - 1 belong to group o. group_slot_task[g, o] is a task t with task_row_position[t] between o * 16 and (o + 1) * 16 - 1.
All inputs are finite; a program needn't handle non-finite values. No bound on the sum of `scores` on one device may be relied on, other than what follows from the above.
Results may differ from the reference program's by a relative error of at most 0.0057.
Values may be sent and summed in bfloat16 or wider, within the bound.
No kernel may reach another device: no remote copies, remote signals or barrier semaphores. Data moves between devices by JAX's collectives and lax.ppermute only.
A program may use at most 64 MiB of HBM per device.

```python
import math
import jax
import jax.numpy as jnp
import numpy as np
from jax import lax

MODEL_WIDTH = 8192
KEY_VALUE_COLUMNS = 2048
ADAPTER_RANK = 64
STEPS = 2
TASK_DEV = 16
ATT_DEV = 256
SLOTS = 8
MOST = 128
TASK_COUNT = 128
ATTEMPTS = 2048


def shared_order(key):
    return jax.random.permutation(jax.random.fold_in(key, 17), TASK_COUNT).astype(jnp.int32)


def draw_task_row_position(key, part):
    return shared_order(key)


def draw_group_slot_task(key, part):
    order = shared_order(key)
    inverse = jnp.argsort(order, stable=True).astype(jnp.int32)
    chosen = jax.random.randint(jax.random.fold_in(key, 29), (SLOTS, SLOTS), 0, TASK_DEV, dtype=jnp.int32)
    last_row = order[TASK_COUNT - 1]
    first_row = order[0]
    chosen = chosen.at[0, last_row // TASK_DEV].set(last_row % TASK_DEV)
    chosen = chosen.at[1, first_row // TASK_DEV].set(first_row % TASK_DEV)
    owners = jnp.arange(SLOTS, dtype=jnp.int32)[None, :]
    return inverse[owners * TASK_DEV + chosen].astype(jnp.int32)


def touch_ends(result, key, least, top_value):
    dims = result.shape
    index_at = [jax.random.randint(jax.random.fold_in(key, axis), (), 0, dims[axis]) for axis in range(len(dims))]
    result = result.at[tuple(index_at)].set(least)
    longest = dims.index(max(dims))
    index_at[longest] = (index_at[longest] + 1) % dims[longest]
    return result.at[tuple(index_at)].set(top_value)


def block_levels(stream_key, extent, shards, smallest, high):
    def one(dim, shards_of):
        heights = jax.random.uniform(jax.random.fold_in(jax.random.fold_in(stream_key, 6), dim), (shards_of,), jnp.float32, smallest / len(shards), high / len(shards))
        return jnp.repeat(jnp.exp(heights), extent[dim] // shards_of).reshape((-1,) + (1,) * (len(extent) - dim - 1))

    factor_of = one(*shards[0])
    for cut in shards[1:]:
        factor_of = factor_of * one(*cut)
    return factor_of


def assign_block(key, own, number, rows, count, top, bound, slope):
    order = jax.random.permutation(key, count)
    heavy_load, usual = shares(count, rows * top, bound, slope, True), shares(count, rows * top, bound, slope, False)
    places = jnp.arange(count)

    def named(tallies, rotation):
        used = int((tallies > 0).sum())
        fixed = max(1, used // 4)
        passed = fixed + (places - fixed + rotation * (used - fixed)) % max(1, count - fixed)
        return jnp.zeros((count,), jnp.int32).at[order[jnp.where(places < fixed, places, passed)]].set(jnp.asarray(tallies, jnp.int32))

    tallies = jnp.where(number % 4 == 0, named(heavy_load, number // 4), named(usual, number - number // 4 - 1))
    mixed = jax.random.permutation(jax.random.fold_in(own, 3), count)
    source_of, taker = mixed[0:count // 2 * 2:2], mixed[1:count // 2 * 2:2]
    slack = jnp.minimum(tallies[source_of] - 1, bound - tallies[taker]) // 2
    slack = jnp.where((source_of == order[0]) | (taker == order[0]) | (tallies[taker] == 0), 0, jnp.maximum(slack, 0))
    passed = jax.random.randint(jax.random.fold_in(own, 4), (count // 2,), 0, 1 << 20) % (slack + 1)
    tallies = tallies.at[source_of].add(-passed).at[taker].add(passed)
    members = jnp.searchsorted(jnp.cumsum(tallies), jnp.arange(rows * top), side="right").astype(jnp.int32)
    grid = members.reshape(top, rows).T
    grid = grid[jax.random.permutation(jax.random.fold_in(own, 1), rows)]
    rotation = jax.random.randint(jax.random.fold_in(own, 2), (rows, 1), 0, top)
    return jnp.take_along_axis(grid, (jnp.arange(top)[None, :] + rotation) % top, axis=1)


def shares(number_of, total, reach, slope, full):
    weights = [(1 << 20) // math.isqrt(rank ** slope) + 1 for rank in range(1, number_of + 1)]
    largest = reach if full else min(reach, max(-(-total // number_of), total * weights[0] // sum(weights)))
    least = 1 if total - largest >= number_of - 1 else 0
    counts, rest = [largest] + [least] * (number_of - 1), total - largest - least * (number_of - 1)
    while rest > 0:
        free = [i for i in range(1, number_of) if counts[i] < largest] or [i for i in range(1, number_of) if counts[i] < reach]
        pool, remaining = sum([weights[i] for i in free]), rest
        for i in free:
            addition = min(reach - counts[i], max(1, remaining * weights[i] // pool), rest)
            counts[i] = counts[i] + addition
            rest = rest - addition
    return np.array(counts)


def bell_draw(rng, dims, scale, limit, cuts=(), kind=jnp.bfloat16):
    values = jax.random.normal(rng, dims, jnp.float32) * scale
    if len(cuts) > 0:
        values = block_levels(rng, dims, cuts, -0.22, 0.18) * values
    return jnp.clip(values, min=-limit, max=limit).astype(kind)


def setup_inputs(seed: int = 0) -> dict:
    seeds = jax.random.split(jax.random.key(seed), 10)
    hidden = bell_draw(seeds[0], (ATTEMPTS, STEPS, MODEL_WIDTH), 1.0, 6.0, ((0, 8), (2, 4)))
    key_value_weight = bell_draw(seeds[1], (MODEL_WIDTH, KEY_VALUE_COLUMNS), MODEL_WIDTH ** -0.5, 0.0625, ((0, 4),))
    adapter_down_weight = bell_draw(seeds[2], (TASK_COUNT, MODEL_WIDTH, ADAPTER_RANK), MODEL_WIDTH ** -0.5, 0.0625, ((0, 8), (1, 4)))
    adapter_up_weight = bell_draw(seeds[3], (TASK_COUNT, ADAPTER_RANK, KEY_VALUE_COLUMNS), ADAPTER_RANK ** -0.5, 0.75, ((0, 8), (2, 4)))
    attempt_adapter_slot_keys = jax.random.split(jax.random.fold_in(seeds[4], 1), ATTEMPTS // ATT_DEV)
    attempt_adapter_slot_turns = jax.random.permutation(jax.random.fold_in(seeds[4], 3), ATTEMPTS // ATT_DEV)
    attempt_adapter_slot = jax.vmap(lambda own, number: assign_block(jax.random.fold_in(seeds[4], 2), own, number, ATT_DEV, SLOTS, 1, MOST, 2))(attempt_adapter_slot_keys, attempt_adapter_slot_turns).reshape((ATTEMPTS, 1))
    group_slot_task = draw_group_slot_task(jax.random.fold_in(seeds[9], 71), 0)
    task_row_position = draw_task_row_position(jax.random.fold_in(seeds[9], 71), 0)
    scores = touch_ends((jax.random.randint(seeds[7], (ATTEMPTS,), 0, 2) < 1).astype(jnp.int32), jax.random.fold_in(seeds[7], 1), 0, 1)
    cotangent = bell_draw(seeds[8], (ATTEMPTS, STEPS, KEY_VALUE_COLUMNS), 1.0, 6.0, ((0, 8), (2, 4)))
    return {"hidden": hidden, "key_value_weight": key_value_weight, "adapter_down_weight": adapter_down_weight, "adapter_up_weight": adapter_up_weight, "attempt_adapter_slot": attempt_adapter_slot, "group_slot_task": group_slot_task, "task_row_position": task_row_position, "scores": scores, "cotangent": cotangent}


adapter_output_scale = 0.25


def reference(hidden, key_value_weight, adapter_down_weight, adapter_up_weight, attempt_adapter_slot, group_slot_task, task_row_position, scores, cotangent):
    group_ids = (jnp.arange(ATTEMPTS, dtype=jnp.int32) // ATT_DEV).astype(jnp.int32)
    slot_of = attempt_adapter_slot[:, 0].astype(jnp.int32)
    task_of = group_slot_task[group_ids, slot_of].astype(jnp.int32)
    score_f = scores.astype(jnp.float32)
    task_sums = jax.ops.segment_sum(score_f, task_of, num_segments=TASK_COUNT)
    task_counts = jax.ops.segment_sum(jnp.ones_like(score_f), task_of, num_segments=TASK_COUNT)
    task_means = task_sums / jnp.maximum(task_counts, 1.0)
    advantage = score_f - task_means[task_of]
    weighted = (advantage[:, None, None] * cotangent.astype(jnp.float32)).astype(jnp.bfloat16)
    base_rows = jnp.dot(hidden.reshape(ATTEMPTS * STEPS, MODEL_WIDTH), key_value_weight, preferred_element_type=jnp.float32)
    base_rows = base_rows.reshape(ATTEMPTS, STEPS, KEY_VALUE_COLUMNS)
    stored = task_row_position[task_of].astype(jnp.int32)

    def per_attempt(carried, pieces):
        grad_a, grad_b = carried
        input_rows, gradient_rows, stored_row_index = pieces
        down_weight_block = lax.dynamic_index_in_dim(adapter_down_weight, stored_row_index, 0, keepdims=False)
        up_weight_block = lax.dynamic_index_in_dim(adapter_up_weight, stored_row_index, 0, keepdims=False)
        inner_down_product = jnp.dot(input_rows, down_weight_block, preferred_element_type=jnp.float32).astype(jnp.bfloat16)
        inner_backward_product = lax.dot_general(gradient_rows, up_weight_block, (((1,), (1,)), ((), ())), preferred_element_type=jnp.float32).astype(jnp.bfloat16)
        adapter_delta_rows = (adapter_output_scale * jnp.dot(inner_down_product, up_weight_block, preferred_element_type=jnp.float32)).astype(jnp.bfloat16)
        added_down_gradient = adapter_output_scale * lax.dot_general(input_rows, inner_backward_product, (((0,), (0,)), ((), ())), preferred_element_type=jnp.float32)
        added_up_gradient = adapter_output_scale * lax.dot_general(inner_down_product, gradient_rows, (((0,), (0,)), ((), ())), preferred_element_type=jnp.float32)
        old_a = lax.dynamic_index_in_dim(grad_a, stored_row_index, 0, keepdims=False)
        old_b = lax.dynamic_index_in_dim(grad_b, stored_row_index, 0, keepdims=False)
        grad_a = lax.dynamic_update_index_in_dim(grad_a, old_a + added_down_gradient, stored_row_index, 0)
        grad_b = lax.dynamic_update_index_in_dim(grad_b, old_b + added_up_gradient, stored_row_index, 0)
        return (grad_a, grad_b), adapter_delta_rows

    start = (jnp.zeros((TASK_COUNT, MODEL_WIDTH, ADAPTER_RANK), jnp.float32), jnp.zeros((TASK_COUNT, ADAPTER_RANK, KEY_VALUE_COLUMNS), jnp.float32))
    (grad_a, grad_b), deltas = lax.scan(per_attempt, start, (hidden, weighted, stored))
    kv_new = (base_rows + deltas.astype(jnp.float32)).astype(jnp.bfloat16)
    return kv_new, grad_a.astype(jnp.bfloat16), grad_b.astype(jnp.bfloat16)
```

```python
import functools

import jax
import jax.numpy as jnp
from jax import lax
from jax.experimental import pallas as pl
from jax.experimental.pallas import tpu as pltpu
from jax.sharding import PartitionSpec as P

scale = 0.25
bf = jnp.bfloat16
f32 = jnp.float32
big = 48 * 1024 * 1024

ANY = pl.BlockSpec(memory_space=pl.ANY)
SMEM = pl.BlockSpec(memory_space=pltpu.SMEM)
VMEM = pl.BlockSpec(memory_space=pltpu.VMEM)


def params():
    return pltpu.CompilerParams(vmem_limit_bytes=big)


def cost(flops, nbytes):
    return pl.CostEstimate(flops=flops, bytes_accessed=nbytes, transcendentals=0)


def nbytes(*arrays):
    return sum(a.size * a.dtype.itemsize for a in arrays)


def swap(x, k, axis):
    n = lax.axis_size(axis)
    return lax.ppermute(x, axis, [(i, i ^ k) for i in range(n)])


def total(x, axis, wire=None):
    k = 1
    while k < lax.axis_size(axis):
        x = x + swap(x if wire is None else x.astype(wire), k, axis).astype(x.dtype)
        k *= 2
    return x


def pack_kernel(groups, tasks, gst, trp, stored, *rest):
    outs, sem = rest[:groups], rest[groups]
    me = lax.axis_index("dp")
    copies = []
    for k in reversed(range(groups)):
        row = lax.rem(trp[gst[me ^ k, me]], tasks)
        copies.append(pltpu.make_async_copy(stored.at[row], outs[k], sem.at[k]))
        copies[-1].start()
    for c in copies:
        c.wait()


def pack(gst, trp, stored):
    groups, tasks = gst.shape[0], stored.shape[0]
    shape = jax.ShapeDtypeStruct(stored.shape[1:], stored.dtype)
    return pl.pallas_call(
        functools.partial(pack_kernel, groups, tasks),
        out_shape=[shape] * groups,
        in_specs=[SMEM, SMEM, ANY],
        out_specs=[ANY] * groups,
        scratch_shapes=[pltpu.SemaphoreType.DMA((groups,))],
        compiler_params=params(),
        cost_estimate=cost(0, 2 * groups * stored.size // tasks * 2),
    )(gst, trp, stored)


def score_kernel(slots, gst, slot, score, out):
    me = lax.axis_index("dp")
    hot = slot[...] == lax.broadcasted_iota(jnp.int32, (slots, slot.shape[1]), 0)
    sums = jnp.sum(jnp.where(hot, score[...].astype(f32), 0.0), axis=1, keepdims=True)
    counts = jnp.sum(jnp.where(hot, 1.0, 0.0), axis=1, keepdims=True)
    lane = lax.broadcasted_iota(jnp.int32, (1, out.shape[1]), 1)
    a = jnp.zeros((1, out.shape[1]), f32)
    b = jnp.zeros((1, out.shape[1]), f32)
    for s in range(slots):
        mine = lane == gst[me, s]
        a += jnp.where(mine, sums[s : s + 1, :], 0.0)
        b += jnp.where(mine, counts[s : s + 1, :], 0.0)
    out[0:1, :] = a
    out[1:2, :] = b


def advantage_kernel(slots, gst, totals, slot, score, out):
    me = lax.axis_index("dp")
    means = totals[0:1, :] / jnp.maximum(totals[1:2, :], 1.0)
    lane = lax.broadcasted_iota(jnp.int32, means.shape, 1)
    mean_of = jnp.zeros(slot.shape, f32)
    for s in range(slots):
        m = jnp.sum(jnp.where(lane == gst[me, s], means, 0.0), axis=1, keepdims=True)
        mean_of += jnp.where(slot[...] == s, m, 0.0)
    out[...] = score[...].astype(f32) - mean_of


def base_kernel(mine, hidden, weight, out):
    out[0] = jnp.dot(hidden[...], weight[...], preferred_element_type=f32).astype(bf)


def base_parts(rows, weight, parts):
    n, width = rows.shape
    cols = weight.shape[1] // parts
    mine = lax.axis_index("tensor").astype(jnp.int32).reshape(1)
    return pl.pallas_call(
        base_kernel,
        out_shape=jax.ShapeDtypeStruct((parts, n, cols), bf),
        grid_spec=pltpu.PrefetchScalarGridSpec(
            num_scalar_prefetch=1,
            grid=(parts,),
            in_specs=[
                pl.BlockSpec((n, width), lambda i, m: (0, 0)),
                pl.BlockSpec((width, cols), lambda i, m: (0, m[0] ^ i)),
            ],
            out_specs=pl.BlockSpec((1, n, cols), lambda i, m: (i, 0, 0)),
        ),
        compiler_params=params(),
        cost_estimate=cost(2 * n * width * weight.shape[1], nbytes(rows, weight)),
    )(mine, rows, weight)


def inner_kernel(groups, place, rows, *rest):
    blocks, out = rest[:groups], rest[groups]
    acc = jnp.zeros(out.shape, f32)
    for k in range(groups):
        part = lax.dot_general(
            blocks[k][...], rows[...], (((1,), (1,)), ((), ())), preferred_element_type=f32
        )
        acc = jnp.where(place[...] == k, part, acc)
    out[...] = acc


def inner(place, rows, blocks):
    rank = blocks[0].shape[0]
    n = rows.shape[0]
    return pl.pallas_call(
        functools.partial(inner_kernel, len(blocks)),
        out_shape=jax.ShapeDtypeStruct((rank, n), f32),
        in_specs=[VMEM] * (2 + len(blocks)),
        out_specs=VMEM,
        compiler_params=params(),
        cost_estimate=cost(2 * n * rows.shape[1] * rank * len(blocks), nbytes(rows, *blocks)),
    )(place, rows, *blocks)


def grad_kernel(groups, place, adv, inner_t, rows, *outs):
    t = (adv[...] * inner_t[...]).astype(bf)
    zero = jnp.zeros((), bf)
    for k in range(groups):
        part = jnp.where(place[...] == k, t, zero)
        outs[k][...] = (
            scale * jnp.dot(part, rows[...], preferred_element_type=f32)
        ).astype(bf)


def grads(place, adv, inner_t, rows, groups):
    rank = inner_t.shape[0]
    n, width = rows.shape
    shape = jax.ShapeDtypeStruct((rank, width), bf)
    return pl.pallas_call(
        functools.partial(grad_kernel, groups),
        out_shape=[shape] * groups,
        in_specs=[VMEM] * 4,
        out_specs=[VMEM] * groups,
        compiler_params=params(),
        cost_estimate=cost(2 * n * width * rank * groups, nbytes(rows) + groups * rank * width * 2),
    )(place, adv, inner_t, rows)


def delta_kernel(groups, place, inner_t, base_mine, base_got, *rest):
    blocks, out = rest[:groups], rest[groups]
    t = inner_t[...].astype(bf)
    zero = jnp.zeros((), bf)
    spread = jnp.concatenate([jnp.where(place[...] == k, t, zero) for k in range(groups)], axis=0)
    ups = jnp.concatenate([b[...] for b in blocks], axis=0)
    delta = lax.dot_general(spread, ups, (((0,), (0,)), ((), ())), preferred_element_type=f32)
    delta = (scale * delta).astype(bf).astype(f32)
    out[...] = (base_mine[...].astype(f32) + base_got[...].astype(f32) + delta).astype(bf)


def adapted(place, inner_t, base_mine, base_got, blocks):
    n, cols = base_got.shape
    groups = len(blocks)
    return pl.pallas_call(
        functools.partial(delta_kernel, groups),
        out_shape=jax.ShapeDtypeStruct((n, cols), bf),
        in_specs=[VMEM] * (4 + groups),
        out_specs=VMEM,
        compiler_params=params(),
        cost_estimate=cost(2 * n * cols * groups * inner_t.shape[0], nbytes(*blocks) + 3 * n * cols * 2),
    )(place, inner_t, base_mine, base_got, *blocks)


def combine_kernel(groups, tasks, gst, trp, *rest):
    blocks, out = rest[:groups], rest[groups]
    me = lax.axis_index("dp")
    here = pl.program_id(0)
    rows = [lax.rem(trp[gst[me ^ k, me]], tasks) for k in range(groups)]
    acc = jnp.zeros(out.shape[1:], f32)
    for k in range(groups):
        acc += jnp.where(rows[k] == here, blocks[k][...].astype(f32), 0.0)
    out[0] = acc.astype(bf)


def combine(gst, trp, blocks, tasks):
    groups = len(blocks)
    rank, width = blocks[0].shape
    return pl.pallas_call(
        functools.partial(combine_kernel, groups, tasks),
        out_shape=jax.ShapeDtypeStruct((tasks, rank, width), bf),
        grid=(tasks,),
        in_specs=[SMEM, SMEM] + [VMEM] * groups,
        out_specs=pl.BlockSpec((1, rank, width), lambda t: (t, 0, 0)),
        compiler_params=params(),
        cost_estimate=cost(0, (groups + tasks) * rank * width * 2),
    )(gst, trp, *blocks)


def body(hidden, weight, down, up, slot, gst, trp, scores, cotangent):
    groups, parts = lax.axis_size("dp"), lax.axis_size("tensor")
    me = lax.axis_index("dp")
    att, steps, width = hidden.shape
    cols = cotangent.shape[2]
    n = att * steps
    tasks = down.shape[0]

    up_out = pack(gst, trp, up)
    down_out = pack(gst, trp, jnp.swapaxes(down, 1, 2))
    order = list(reversed(range(1, groups)))
    up_in = [up_out[0]] + [None] * (groups - 1)
    down_in = [down_out[0]] + [None] * (groups - 1)
    for k in order:
        up_in[k] = swap(up_out[k], k, "dp")
    for k in order:
        down_in[k] = swap(down_out[k], k, "dp")

    slot_row = slot.reshape(1, att)
    score_row = scores.reshape(1, att)
    local = pl.pallas_call(
        functools.partial(score_kernel, groups),
        out_shape=jax.ShapeDtypeStruct((2, trp.shape[0]), f32),
        in_specs=[SMEM, VMEM, VMEM],
        out_specs=VMEM,
    )(gst, slot_row, score_row)
    totals = total(local, "dp")
    slot_rows = jnp.repeat(slot_row, steps, axis=1)
    score_rows = jnp.repeat(score_row, steps, axis=1)
    place = slot_rows ^ me
    adv = pl.pallas_call(
        functools.partial(advantage_kernel, groups),
        out_shape=jax.ShapeDtypeStruct((1, n), f32),
        in_specs=[SMEM, VMEM, VMEM, VMEM],
        out_specs=VMEM,
    )(gst, totals, slot_rows, score_rows)

    cot = cotangent.reshape(n, cols)
    rows = hidden.reshape(n, width)

    base = base_parts(rows, weight, parts)
    held = [base[i] for i in range(parts)]
    k = 1
    while 2 * k < parts:
        got = swap(jnp.stack(held[1::2]), k, "tensor")
        held = [
            (a.astype(f32) + got[i].astype(f32)).astype(bf) for i, a in enumerate(held[0::2])
        ]
        k *= 2
    base_mine, base_got = held[0], swap(held[1], k, "tensor")

    back = total(inner(place, cot, up_in), "tensor")
    grad_down_out = grads(place, adv, back, rows, groups)
    grad_down_in = [grad_down_out[0]] + [None] * (groups - 1)
    for k in order:
        grad_down_in[k] = swap(grad_down_out[k], k, "dp")

    ahead = total(inner(place, rows, down_in), "tensor")
    grad_up_out = grads(place, adv, ahead, cot, groups)
    grad_up_in = [grad_up_out[0]] + [None] * (groups - 1)
    for k in order:
        grad_up_in[k] = swap(grad_up_out[k], k, "dp")
    kv_new = adapted(place, ahead, base_mine, base_got, up_in).reshape(att, steps, cols)

    grad_down = jnp.swapaxes(combine(gst, trp, grad_down_in, tasks), 1, 2)
    grad_up = combine(gst, trp, grad_up_in, tasks)
    return (kv_new, grad_down, grad_up)


def solution(mesh):
    in_specs = (
        P("dp", None, "tensor"),
        P("tensor", None),
        P("dp", "tensor", None),
        P("dp", None, "tensor"),
        P("dp", None),
        P(),
        P(),
        P("dp"),
        P("dp", None, "tensor"),
    )
    out_specs = (P("dp", None, "tensor"), P("dp", "tensor", None), P("dp", None, "tensor"))
    return jax.shard_map(body, mesh=mesh, in_specs=in_specs, out_specs=out_specs, check_vma=False)
```

```python
import functools

import jax
import jax.numpy as jnp
from jax import lax
from jax.experimental import pallas as pl
from jax.experimental.pallas import tpu as pltpu
from jax.sharding import PartitionSpec as P

scale = 0.25
bf = jnp.bfloat16
f32 = jnp.float32
big = 63 * 1024 * 1024
spare = 16

ANY = pl.BlockSpec(memory_space=pl.ANY)
SMEM = pl.BlockSpec(memory_space=pltpu.SMEM)
VMEM = pl.BlockSpec(memory_space=pltpu.VMEM)


def shaped(shape, dtype):
    return jax.ShapeDtypeStruct(shape, dtype)


def call(kernel, outs, operands, specs, flops=0, scratch=(), after=(), vmem_outs=True):
    moved = sum(a.size * a.dtype.itemsize for a in list(operands) + list(outs))
    count = len(operands)

    def run(*refs):
        kernel(refs[:count], refs[count + len(after) :])

    return pl.pallas_call(
        run,
        out_shape=list(outs),
        in_specs=list(specs) + [ANY] * len(after),
        out_specs=[VMEM] * len(outs),
        scratch_shapes=list(scratch),
        compiler_params=pltpu.CompilerParams(vmem_limit_bytes=big),
        cost_estimate=pl.CostEstimate(flops=flops, bytes_accessed=moved, transcendentals=0),
    )(*operands, *after)


def swap(x, k, axis):
    n = lax.axis_size(axis)
    return lax.ppermute(x, axis, [(i, i ^ k) for i in range(n)])


def stored_row(gst, trp, tasks, k):
    me = lax.axis_index("dp")
    return lax.rem(trp[gst[me ^ k, me]], tasks)


def pack_up(gst, trp, up, slot_row, score_row):
    groups = gst.shape[0]
    tasks, rank, cols = up.shape

    def kernel(ins, outs):
        gst, trp, up, slot, score = ins
        sem = outs[-1]
        copies = []
        for k in reversed(range(groups)):
            row = stored_row(gst, trp, tasks, k)
            copies.append(
                pltpu.make_async_copy(up.at[row], outs[k].at[pl.ds(0, rank), :], sem.at[k])
            )
            copies[-1].start()
        hot = slot[...] == lax.broadcasted_iota(jnp.int32, (groups, slot.shape[1]), 0)
        sums = jnp.sum(jnp.where(hot, score[...].astype(f32), 0.0), axis=1, keepdims=True)
        counts = jnp.sum(jnp.where(hot, 1.0, 0.0), axis=1, keepdims=True)
        here = lax.broadcasted_iota(jnp.int32, (groups, cols), 0) == lax.broadcasted_iota(
            jnp.int32, (groups, cols), 1
        )
        sums = jnp.sum(jnp.where(here, sums, 0.0), axis=0, keepdims=True)
        counts = jnp.sum(jnp.where(here, counts, 0.0), axis=0, keepdims=True)
        line = lax.broadcasted_iota(jnp.int32, (spare, cols), 0)
        both = jnp.where(line == 0, sums, jnp.where(line == 1, counts, 0.0)).astype(bf)
        for k in range(groups):
            outs[k][rank:, :] = both
        for c in copies:
            c.wait()

    return call(
        kernel,
        [shaped((rank + spare, cols), bf)] * groups,
        (gst, trp, up, slot_row, score_row),
        [SMEM, SMEM, ANY, VMEM, VMEM],
        scratch=[pltpu.SemaphoreType.DMA((groups,))],
    )


def pack_down(gst, trp, down, after):
    groups = gst.shape[0]
    tasks, rank, width = down.shape

    def kernel(ins, outs):
        gst, trp, down = ins
        out, sem = outs
        me = lax.axis_index("dp")
        copies = []
        for g in range(groups):
            row = lax.rem(trp[gst[g, me]], tasks)
            copies.append(pltpu.make_async_copy(down.at[row], out.at[g], sem.at[g]))
            copies[-1].start()
        for c in copies:
            c.wait()

    return call(
        kernel,
        [shaped((groups, rank, width), bf)],
        (gst, trp, down),
        [SMEM, SMEM, ANY],
        scratch=[pltpu.SemaphoreType.DMA((groups,))],
        after=after,
    )[0]


def base_parts(rows, weight, parts, after):
    n, width = rows.shape
    cols = weight.shape[1] // parts
    mine = lax.axis_index("tensor").astype(jnp.int32).reshape(1)

    def kernel(mine, rows, weight, *rest):
        rest[-1][0] = jnp.dot(rows[...], weight[...], preferred_element_type=f32).astype(bf)

    return pl.pallas_call(
        kernel,
        out_shape=shaped((parts, n, cols), bf),
        grid_spec=pltpu.PrefetchScalarGridSpec(
            num_scalar_prefetch=1,
            grid=(parts,),
            in_specs=[
                pl.BlockSpec((n, width), lambda i, m: (0, 0)),
                pl.BlockSpec((width, cols), lambda i, m: (0, m[0] ^ i)),
            ]
            + [ANY] * len(after),
            out_specs=pl.BlockSpec((1, n, cols), lambda i, m: (i, 0, 0)),
        ),
        compiler_params=pltpu.CompilerParams(vmem_limit_bytes=big),
        cost_estimate=pl.CostEstimate(
            flops=2 * n * width * weight.shape[1],
            bytes_accessed=2 * (rows.size + weight.size + n * weight.shape[1]),
            transcendentals=0,
        ),
    )(mine, rows, weight, *after)


def inner_up(place, rows, blocks, after):
    rank = blocks[0].shape[0] - spare
    n, cols = rows.shape

    def kernel(ins, outs):
        place, rows = ins[:2]
        acc = jnp.zeros((rank, n), f32)
        for k, block in enumerate(ins[2:]):
            part = lax.dot_general(
                block[:rank, :], rows[...], (((1,), (1,)), ((), ())), preferred_element_type=f32
            )
            acc = jnp.where(place[...] == k, part, acc)
        outs[0][...] = acc

    operands = (place, rows, *blocks)
    return call(
        kernel,
        [shaped((rank, n), f32)],
        operands,
        [VMEM] * len(operands),
        flops=2 * n * cols * rank * len(blocks),
        after=after,
    )[0]


def inner_down(slot_rows, rows, blocks, after):
    groups, rank, width = blocks.shape
    n = rows.shape[0]

    def kernel(ins, outs):
        slot, rows, blocks = ins
        acc = jnp.zeros((rank, n), f32)
        for s in range(groups):
            part = lax.dot_general(
                blocks[s], rows[...], (((1,), (1,)), ((), ())), preferred_element_type=f32
            )
            acc = jnp.where(slot[...] == s, part, acc)
        outs[0][...] = acc

    return call(
        kernel,
        [shaped((rank, n), f32)],
        (slot_rows, rows, blocks),
        [VMEM] * 3,
        flops=2 * n * width * rank * groups,
        after=after,
    )[0]


def sum_first(x, axis):
    k = 1
    while 2 * k < lax.axis_size(axis):
        x = x + swap(x, k, axis)
        k *= 2
    return x, swap(x, k, axis)


def spread(place, inner_t, k):
    return jnp.where(place == k, inner_t, jnp.zeros((), inner_t.dtype))


def down_grads(gst, slot_rows, score_rows, t, t_got, rows, up_blocks):
    groups = len(up_blocks)
    rank, n = t.shape
    width = rows.shape[1]

    def kernel(ins, outs):
        gst, slot, score, t, t_got, rows = ins[:6]
        me = lax.axis_index("dp")
        mine = gst[pl.ds(me, 1), :]
        sums = jnp.zeros((1, groups), f32)
        counts = jnp.zeros((1, groups), f32)
        for k, block in enumerate(ins[6:]):
            same = gst[pl.ds(me ^ k, 1), :] == mine
            x = block[rank:, :].astype(f32)
            sums += jnp.where(same, x[0:1, :groups], 0.0)
            counts += jnp.where(same, x[1:2, :groups], 0.0)
        mean = sums / jnp.maximum(counts, 1.0)
        here = lax.broadcasted_iota(jnp.int32, (groups, groups), 0) == lax.broadcasted_iota(
            jnp.int32, (groups, groups), 1
        )
        mean = jnp.sum(jnp.where(here, mean, 0.0), axis=1, keepdims=True)
        hot = slot[...] == lax.broadcasted_iota(jnp.int32, (groups, n), 0)
        adv = score[...].astype(f32) - jnp.sum(jnp.where(hot, mean, 0.0), axis=0, keepdims=True)
        total = (adv * (t[...] + t_got[...])).astype(bf)
        outs[0][...] = adv
        for s in range(groups):
            part = spread(slot[...], total, s)
            outs[1][s] = (scale * jnp.dot(part, rows[...], preferred_element_type=f32)).astype(bf)

    operands = (gst, slot_rows, score_rows, t, t_got, rows, *up_blocks)
    return call(
        kernel,
        [shaped((1, n), f32), shaped((groups, rank, width), bf)],
        operands,
        [VMEM] * len(operands),
        flops=2 * n * width * rank * groups,
    )


def up_grads(place, adv, t, t_got, cot, groups):
    rank, n = t.shape
    cols = cot.shape[1]

    def kernel(ins, outs):
        place, adv, t, t_got, cot = ins
        total = t[...] + t_got[...]
        outs[0][...] = total.astype(bf)
        total = (adv[...] * total).astype(bf)
        for k in range(groups):
            part = spread(place[...], total, k)
            outs[1 + k][...] = (
                scale * jnp.dot(part, cot[...], preferred_element_type=f32)
            ).astype(bf)

    out = call(
        kernel,
        [shaped((rank, n), bf)] + [shaped((rank, cols), bf)] * groups,
        (place, adv, t, t_got, cot),
        [VMEM] * 5,
        flops=2 * n * cols * rank * groups,
    )
    return out[0], out[1:]


def adapted(place, inner_t, base_mine, base_got, blocks, after):
    n, cols = base_got.shape
    rank = inner_t.shape[0]

    def kernel(ins, outs):
        place, t, base_mine, base_got = ins[:4]
        blocks = ins[4:]
        wide = jnp.concatenate([spread(place[...], t[...], k) for k in range(len(blocks))], axis=0)
        ups = jnp.concatenate([b[:rank, :] for b in blocks], axis=0)
        delta = lax.dot_general(wide, ups, (((0,), (0,)), ((), ())), preferred_element_type=f32)
        delta = (scale * delta).astype(bf).astype(f32)
        outs[0][...] = (base_mine[...].astype(f32) + base_got[...].astype(f32) + delta).astype(bf)

    operands = (place, inner_t, base_mine, base_got, *blocks)
    return call(
        kernel,
        [shaped((n, cols), bf)],
        operands,
        [VMEM] * len(operands),
        flops=2 * n * cols * rank * len(blocks),
        after=after,
    )[0]


def combine(gst, trp, blocks, tasks, stacked, after):
    groups = gst.shape[0]
    rank, width = blocks[0].shape[-2:]
    chunk = 4 if tasks % 4 == 0 else 1

    def run(gst, trp, *refs):
        ins = refs[: len(blocks)]
        out, acc = refs[-2:]
        me = lax.axis_index("dp")
        rows = [
            lax.rem(trp[gst[g if stacked else me ^ g, me]], tasks) for g in range(groups)
        ]
        read = [ins[0].at[g] if stacked else ins[g] for g in range(groups)]
        for j in range(chunk):
            here = pl.program_id(0) * chunk + j
            hits = jnp.int32(0)
            for r in rows:
                hits += (r == here).astype(jnp.int32)

            @pl.when(hits == 0)
            def _():
                out[j] = jnp.zeros((rank, width), bf)

            @pl.when(hits == 1)
            def _():
                for g, r in enumerate(rows):

                    @pl.when(r == here)
                    def _():
                        out[j] = read[g][...]

            @pl.when(hits > 1)
            def _():
                acc[...] = jnp.zeros((rank, width), f32)
                for g, r in enumerate(rows):

                    @pl.when(r == here)
                    def _():
                        acc[...] += read[g][...].astype(f32)

                out[j] = acc[...].astype(bf)

    return pl.pallas_call(
        run,
        out_shape=shaped((tasks, rank, width), bf),
        grid=(tasks // chunk,),
        in_specs=[SMEM, SMEM] + [VMEM] * len(blocks) + [ANY] * len(after),
        out_specs=pl.BlockSpec((chunk, rank, width), lambda t: (t, 0, 0)),
        scratch_shapes=[pltpu.VMEM((rank, width), f32)],
        compiler_params=pltpu.CompilerParams(vmem_limit_bytes=big),
        cost_estimate=pl.CostEstimate(
            flops=0,
            bytes_accessed=2 * (groups + tasks) * rank * width,
            transcendentals=0,
        ),
    )(gst, trp, *blocks, *after)


def exchange(x):
    return lax.all_to_all(x, "dp", split_axis=0, concat_axis=0, tiled=True)


def body(hidden, weight, down, up, slot, gst, trp, scores, cotangent):
    groups, parts = lax.axis_size("dp"), lax.axis_size("tensor")
    me = lax.axis_index("dp")
    att, steps, width = hidden.shape
    cols = cotangent.shape[2]
    n = att * steps
    tasks = down.shape[0]
    down = jnp.swapaxes(down, 1, 2)

    slot_row = slot.reshape(1, att)
    score_row = scores.reshape(1, att)
    up_out = pack_up(gst, trp, up, slot_row, score_row)
    up_got = [up_out[0]] + [swap(up_out[k], k, "dp") for k in range(1, groups)]
    down_out = pack_down(gst, trp, down, (up_out[0],))
    down_got = exchange(lax.optimization_barrier((down_out, *up_got))[0])

    hidden, cotangent, slot_row, score_row, _ = lax.optimization_barrier(
        (hidden, cotangent, slot_row, score_row, down_out)
    )
    slot_rows = jnp.repeat(slot_row, steps, axis=1)
    score_rows = jnp.repeat(score_row, steps, axis=1)
    place = slot_rows ^ me
    cot = cotangent.reshape(n, cols)
    rows = hidden.reshape(n, width)

    base = base_parts(rows, weight, parts, (down_out,))
    held = [base[i] for i in range(parts)]
    k = 1
    while 2 * k < parts:
        got = swap(jnp.stack(held[1::2]), k, "tensor")
        held = [
            (a.astype(f32) + got[i].astype(f32)).astype(bf) for i, a in enumerate(held[0::2])
        ]
        k *= 2
    base_mine, base_got = held[0], swap(held[1], k, "tensor")

    back = inner_up(place, cot, up_got, (base,))
    back, back_got = sum_first(back, "tensor")
    adv, down_grad = down_grads(gst, slot_rows, score_rows, back, back_got, rows, up_got)
    down_grad_got = exchange(down_grad)

    ahead = inner_down(slot_rows, rows, down_got, (adv,))
    ahead, ahead_got = sum_first(ahead, "tensor")
    inner_all, up_grad = up_grads(place, adv, ahead, ahead_got, cot, groups)
    up_grad_got = [up_grad[0]] + [swap(up_grad[k], k, "dp") for k in range(1, groups)]
    kv_new = adapted(place, inner_all, base_mine, base_got, up_got, (up_grad[0],))
    kv_out = kv_new.reshape(att, steps, cols)

    grad_down = combine(gst, trp, [down_grad_got], tasks, True, (kv_new,))
    grad_up = combine(gst, trp, up_grad_got, tasks, False, (grad_down,))
    return (kv_out, jnp.swapaxes(grad_down, 1, 2), grad_up)


def solution(mesh):
    in_specs = (
        P("dp", None, "tensor"),
        P("tensor", None),
        P("dp", "tensor", None),
        P("dp", None, "tensor"),
        P("dp", None),
        P(),
        P(),
        P("dp"),
        P("dp", None, "tensor"),
    )
    out_specs = (P("dp", None, "tensor"), P("dp", "tensor", None), P("dp", None, "tensor"))
    return jax.shard_map(body, mesh=mesh, in_specs=in_specs, out_specs=out_specs, check_vma=False)
```

```python
import functools

import jax
import jax.numpy as jnp
from jax import lax
from jax.experimental import pallas as pl
from jax.experimental.pallas import tpu as pltpu
from jax.sharding import PartitionSpec as P

scale = 0.25
bf = jnp.bfloat16
f32 = jnp.float32
big = 64 * 1024 * 1024
spare = 16
lanes = 128

ANY = pl.BlockSpec(memory_space=pl.ANY)
SMEM = pl.BlockSpec(memory_space=pltpu.SMEM)
VMEM = pl.BlockSpec(memory_space=pltpu.VMEM)


def shaped(shape, dtype):
    return jax.ShapeDtypeStruct(shape, dtype)


def call(kernel, outs, operands, specs, flops=0, scratch=(), after=(), vmem_outs=True):
    moved = sum(a.size * a.dtype.itemsize for a in list(operands) + list(outs))
    count = len(operands)

    def run(*refs):
        kernel(refs[:count], refs[count + len(after) :])

    return pl.pallas_call(
        run,
        out_shape=list(outs),
        in_specs=list(specs) + [ANY] * len(after),
        out_specs=[VMEM] * len(outs),
        scratch_shapes=list(scratch),
        compiler_params=pltpu.CompilerParams(vmem_limit_bytes=big),
        cost_estimate=pl.CostEstimate(flops=0, bytes_accessed=0, transcendentals=0),
    )(*operands, *after)


def swap(x, k, axis):
    n = lax.axis_size(axis)
    return lax.ppermute(x, axis, [(i, i ^ k) for i in range(n)])


def stored_row(gst, trp, tasks, k):
    me = lax.axis_index("dp")
    return lax.rem(trp[gst[me ^ k, me]], tasks)


def pack_up(gst, trp, up, slot_row, score_row):
    groups = gst.shape[0]
    tasks, rank, cols = up.shape
    tiles = cols // lanes

    def kernel(ins, outs):
        gst, trp, up, slot, score = ins
        sem = outs[-1]
        copies = []
        for k in reversed(range(groups)):
            row = stored_row(gst, trp, tasks, k)
            for j in range(tiles):
                copies.append(
                    pltpu.make_async_copy(
                        up.at[row, :, pl.ds(j * lanes, lanes)],
                        outs[k].at[pl.ds(j * rank, rank), :],
                        sem.at[k, j],
                    )
                )
                copies[-1].start()
        hot = slot[...] == lax.broadcasted_iota(jnp.int32, (groups, slot.shape[1]), 0)
        sums = jnp.sum(jnp.where(hot, score[...].astype(f32), 0.0), axis=1, keepdims=True)
        counts = jnp.sum(jnp.where(hot, 1.0, 0.0), axis=1, keepdims=True)
        here = lax.broadcasted_iota(jnp.int32, (groups, lanes), 0) == lax.broadcasted_iota(
            jnp.int32, (groups, lanes), 1
        )
        sums = jnp.sum(jnp.where(here, sums, 0.0), axis=0, keepdims=True)
        counts = jnp.sum(jnp.where(here, counts, 0.0), axis=0, keepdims=True)
        line = lax.broadcasted_iota(jnp.int32, (spare, lanes), 0)
        both = jnp.where(line == 0, sums, jnp.where(line == 1, counts, 0.0)).astype(bf)
        for k in range(groups):
            outs[k][tiles * rank :, :] = both
        for c in copies:
            c.wait()

    return call(
        kernel,
        [shaped((tiles * rank + spare, lanes), bf)] * groups,
        (gst, trp, up, slot_row, score_row),
        [SMEM, SMEM, ANY, VMEM, VMEM],
        scratch=[pltpu.SemaphoreType.DMA((groups, tiles))],
    )


def up_block(block, rank):
    tiles = block.shape[0] // rank
    return jnp.concatenate([block[j * rank : (j + 1) * rank, :] for j in range(tiles)], axis=1)


def pack_down(gst, trp, down, after):
    groups = gst.shape[0]
    tasks, rank, width = down.shape

    def kernel(ins, outs):
        gst, trp, down = ins
        out, sem = outs
        me = lax.axis_index("dp")
        copies = []
        for g in range(groups):
            row = lax.rem(trp[gst[g, me]], tasks)
            copies.append(pltpu.make_async_copy(down.at[row], out.at[g], sem.at[g]))
            copies[-1].start()
        for c in copies:
            c.wait()

    return call(
        kernel,
        [shaped((groups, rank, width), bf)],
        (gst, trp, down),
        [SMEM, SMEM, ANY],
        scratch=[pltpu.SemaphoreType.DMA((groups,))],
        after=after,
    )[0]


def base_parts(rows, weight, parts, after):
    n, width = rows.shape
    cols = weight.shape[1] // parts
    mine = lax.axis_index("tensor").astype(jnp.int32).reshape(1)

    tiles = 1
    tile = cols // tiles

    def kernel(mine, rows, weight, *rest):
        rest[-1][0] = jnp.dot(rows[...], weight[...], preferred_element_type=f32).astype(bf)

    return pl.pallas_call(
        kernel,
        out_shape=shaped((parts, n, cols), bf),
        grid_spec=pltpu.PrefetchScalarGridSpec(
            num_scalar_prefetch=1,
            grid=(parts, tiles),
            in_specs=[
                pl.BlockSpec((n, width), lambda i, j, m: (0, 0)),
                pl.BlockSpec((width, tile), lambda i, j, m: (0, (m[0] ^ i) * tiles + j)),
            ]
            + [ANY] * len(after),
            out_specs=pl.BlockSpec((1, n, tile), lambda i, j, m: (i, 0, j)),
        ),
        compiler_params=pltpu.CompilerParams(vmem_limit_bytes=big),
        cost_estimate=pl.CostEstimate(
            flops=2 * n * width * weight.shape[1],
            bytes_accessed=2 * (rows.size + weight.size + n * weight.shape[1]),
            transcendentals=0,
        ),
    )(mine, rows, weight, *after)


def inner_up(place, rows, blocks, rank, after):
    n, cols = rows.shape

    def kernel(ins, outs):
        place, rows = ins[:2]
        wide = lax.dot_general(
            jnp.concatenate([up_block(block, rank) for block in ins[2:]], axis=0),
            rows[...],
            (((1,), (1,)), ((), ())),
            preferred_element_type=f32,
        )
        acc = jnp.zeros((rank, n), f32)
        for k in range(len(blocks)):
            acc = jnp.where(place[...] == k, wide[k * rank : (k + 1) * rank], acc)
        outs[0][...] = acc
        outs[1][...] = acc.astype(bf)

    operands = (place, rows, *blocks)
    return call(
        kernel,
        [shaped((rank, n), f32), shaped((rank, n), bf)],
        operands,
        [VMEM] * len(operands),
        flops=2 * n * cols * rank * len(blocks),
        after=after,
    )


def inner_down(slot_rows, rows, blocks, after):
    groups, rank, width = blocks.shape
    n = rows.shape[0]

    def kernel(ins, outs):
        slot, rows, blocks = ins
        wide = lax.dot_general(
            blocks[...].reshape(groups * rank, width),
            rows[...],
            (((1,), (1,)), ((), ())),
            preferred_element_type=f32,
        )
        acc = jnp.zeros((rank, n), f32)
        for s in range(groups):
            acc = jnp.where(slot[...] == s, wide[s * rank : (s + 1) * rank], acc)
        outs[0][...] = acc
        outs[1][...] = acc.astype(bf)

    return call(
        kernel,
        [shaped((rank, n), f32), shaped((rank, n), bf)],
        (slot_rows, rows, blocks),
        [VMEM] * 3,
        flops=2 * n * width * rank * groups,
        after=after,
    )


def plus(x, got):
    def kernel(ins, outs):
        total = ins[0][...] + ins[1][...].astype(f32)
        outs[0][...] = total
        outs[1][...] = total.astype(bf)

    return call(kernel, [shaped(x.shape, f32), shaped(x.shape, bf)], (x, got), [VMEM] * 2)


def sum_first(x, wire, axis):
    k = 1
    while 2 * k < lax.axis_size(axis):
        x, wire = plus(x, swap(wire, k, axis))
        k *= 2
    return x, swap(wire, k, axis)


def spread(place, inner_t, k):
    return jnp.where(place == k, inner_t, jnp.zeros((), inner_t.dtype))


def down_grads(gst, place, slot_rows, score_rows, t, t_got, rows, up_blocks, early):
    groups = len(up_blocks)
    rank, n = t.shape
    width = rows.shape[1]

    def kernel(ins, outs):
        gst, place, slot, score, t, t_got, rows = ins[:7]
        me = lax.axis_index("dp")
        mine = gst[pl.ds(me, 1), :]
        sums = jnp.zeros((1, groups), f32)
        counts = jnp.zeros((1, groups), f32)
        for k, block in enumerate(ins[7:]):
            same = gst[pl.ds(me ^ k, 1), :] == mine
            x = block[block.shape[0] - spare :, :].astype(f32)
            sums += jnp.where(same, x[0:1, :groups], 0.0)
            counts += jnp.where(same, x[1:2, :groups], 0.0)
        mean = sums / jnp.maximum(counts, 1.0)
        here = lax.broadcasted_iota(jnp.int32, (groups, groups), 0) == lax.broadcasted_iota(
            jnp.int32, (groups, groups), 1
        )
        mean = jnp.sum(jnp.where(here, mean, 0.0), axis=1, keepdims=True)
        hot = slot[...] == lax.broadcasted_iota(jnp.int32, (groups, n), 0)
        adv = score[...].astype(f32) - jnp.sum(jnp.where(hot, mean, 0.0), axis=0, keepdims=True)
        total = (adv * (t[...] + t_got[...].astype(f32))).astype(bf)
        outs[0][...] = adv
        wide = jnp.concatenate([spread(place[...], total, k) for k in range(groups)], axis=0)
        part = jnp.dot(wide, rows[:, :early], preferred_element_type=f32)
        part = (scale * part).astype(bf)
        for k in range(groups):
            outs[2 + k][...] = part[k * rank : (k + 1) * rank]
        wide = jnp.concatenate([spread(slot[...], total, s) for s in range(groups)], axis=0)
        part = jnp.dot(wide, rows[:, early:], preferred_element_type=f32)
        outs[1][...] = (scale * part).astype(bf).reshape(groups, rank, width - early)

    operands = (gst, place, slot_rows, score_rows, t, t_got, rows, *up_blocks)
    out = call(
        kernel,
        [shaped((1, n), f32), shaped((groups, rank, width - early), bf)]
        + [shaped((rank, early), bf)] * groups,
        operands,
        [VMEM] * len(operands),
        flops=2 * n * width * rank * groups,
    )
    return out[0], out[1], out[2:]


def up_grads(place, adv, t, t_got, cot, groups):
    rank, n = t.shape
    cols = cot.shape[1]

    def kernel(ins, outs):
        place, adv, t, t_got, cot = ins
        total = t[...] + t_got[...].astype(f32)
        outs[0][...] = total.astype(bf)
        total = (adv[...] * total).astype(bf)
        wide = jnp.concatenate([spread(place[...], total, k) for k in range(groups)], axis=0)
        part = (scale * jnp.dot(wide, cot[...], preferred_element_type=f32)).astype(bf)
        for k in range(groups):
            outs[1 + k][...] = part[k * rank : (k + 1) * rank]

    out = call(
        kernel,
        [shaped((rank, n), bf)] + [shaped((rank, cols), bf)] * groups,
        (place, adv, t, t_got, cot),
        [VMEM] * 5,
        flops=2 * n * cols * rank * groups,
    )
    return out[0], out[1:]


def adapted(place, inner_t, base_mine, base_got, blocks, after):
    n, cols = base_got.shape
    rank = inner_t.shape[0]

    def kernel(ins, outs):
        place, t, base_mine, base_got = ins[:4]
        blocks = ins[4:]
        wide = jnp.concatenate([spread(place[...], t[...], k) for k in range(len(blocks))], axis=0)
        ups = jnp.concatenate([up_block(b, rank) for b in blocks], axis=0)
        delta = lax.dot_general(wide, ups, (((0,), (0,)), ((), ())), preferred_element_type=f32)
        delta = (scale * delta).astype(bf).astype(f32)
        outs[0][...] = (base_mine[...].astype(f32) + base_got[...].astype(f32) + delta).astype(bf)

    operands = (place, inner_t, base_mine, base_got, *blocks)
    return call(
        kernel,
        [shaped((n, cols), bf)],
        operands,
        [VMEM] * len(operands),
        flops=2 * n * cols * rank * len(blocks),
        after=after,
    )[0]


def zeros(shape, after):
    def kernel(refs):
        refs[-1][...] = jnp.zeros(refs[-1].shape, bf)

    chunk = 4 if shape[0] % 4 == 0 else 1
    return pl.pallas_call(
        lambda *refs: kernel(refs),
        out_shape=shaped(shape, bf),
        grid=(shape[0] // chunk,),
        in_specs=[ANY] * len(after),
        out_specs=pl.BlockSpec((chunk,) + shape[1:], lambda t: (t, 0, 0)),
        compiler_params=pltpu.CompilerParams(vmem_limit_bytes=big),
        cost_estimate=pl.CostEstimate(flops=0, bytes_accessed=0, transcendentals=0),
    )(*after)


def combine(gst, trp, blocks, rest, filled, after):
    groups = gst.shape[0]
    tasks, rank, width = filled.shape
    count = len(blocks) + len(rest)
    early = blocks[0].shape[1]

    def kernel(*refs):
        gst, trp = refs[:2]
        ins = refs[2 : 2 + count]
        out, held, acc, sem_in, sem_out = refs[-5:]
        me = lax.axis_index("dp")
        copies = []
        for k in range(groups):
            parts = [pltpu.make_async_copy(ins[k], held.at[k, :, pl.ds(0, early)], sem_in.at[0, k])]
            if rest:
                place = held.at[k, :, pl.ds(early, width - early)]
                parts.append(pltpu.make_async_copy(ins[groups].at[me ^ k], place, sem_in.at[1, k]))
            for c in parts:
                c.start()
            copies.append(parts)
        rows = [stored_row(gst, trp, tasks, k) for k in range(groups)]
        back = [
            pltpu.make_async_copy(held.at[g], out.at[rows[g]], sem_out.at[g])
            for g in range(groups)
        ]
        last = []
        for g in range(groups):
            ends, again = jnp.bool_(True), jnp.bool_(False)
            for h in range(groups):
                if h > g:
                    ends = jnp.logical_and(ends, rows[h] != rows[g])
                if h < g:
                    again = jnp.logical_or(again, rows[h] == rows[g])
            last.append(ends)
            for c in copies[g]:
                c.wait()

            @pl.when(jnp.logical_and(ends, again))
            def _():
                acc[...] = held[g].astype(f32)
                for h in range(g):

                    @pl.when(rows[h] == rows[g])
                    def _():
                        acc[...] += held[h].astype(f32)

                held[g] = acc[...].astype(bf)

            @pl.when(ends)
            def _():
                back[g].start()

        for g in range(groups):

            @pl.when(last[g])
            def _():
                back[g].wait()

    return pl.pallas_call(
        kernel,
        out_shape=shaped(filled.shape, bf),
        in_specs=[SMEM, SMEM] + [ANY] * (count + 1 + len(after)),
        out_specs=ANY,
        scratch_shapes=[
            pltpu.VMEM((groups, rank, width), bf),
            pltpu.VMEM((rank, width), f32),
            pltpu.SemaphoreType.DMA((2, groups)),
            pltpu.SemaphoreType.DMA((groups,)),
        ],
        input_output_aliases={2 + count: 0},
        compiler_params=pltpu.CompilerParams(vmem_limit_bytes=big),
        cost_estimate=pl.CostEstimate(flops=0, bytes_accessed=0, transcendentals=0),
    )(gst, trp, *blocks, *rest, filled, *after)


def exchange(x):
    return lax.all_to_all(x, "dp", split_axis=0, concat_axis=0, tiled=True)


def partners(blocks):
    got = {k: swap(blocks[k], k, "dp") for k in reversed(range(1, len(blocks)))}
    return [blocks[0]] + [got[k] for k in range(1, len(blocks))]


def body(hidden, weight, down, up, slot, gst, trp, scores, cotangent):
    groups, parts = lax.axis_size("dp"), lax.axis_size("tensor")
    me = lax.axis_index("dp")
    att, steps, width = hidden.shape
    cols = cotangent.shape[2]
    n = att * steps
    tasks, rank = down.shape[0], down.shape[2]
    down = jnp.swapaxes(down, 1, 2)

    slot_row = slot.reshape(1, att)
    score_row = scores.reshape(1, att)
    up_out = pack_up(gst, trp, up, slot_row, score_row)
    up_got = partners(up_out)
    down_out = pack_down(gst, trp, down, (up_out[0],))
    down_got = exchange(lax.optimization_barrier((down_out, *up_got))[0])

    hidden, cotangent, slot_row, score_row, _ = lax.optimization_barrier(
        (hidden, cotangent, slot_row, score_row, up_out[0])
    )
    slot_rows = jnp.repeat(slot_row, steps, axis=1)
    score_rows = jnp.repeat(score_row, steps, axis=1)
    place = slot_rows ^ me
    cot = cotangent.reshape(n, cols)
    rows = hidden.reshape(n, width)

    back, back_wire = inner_up(place, cot, up_got, rank, ())
    back, back_got = sum_first(back, back_wire, "tensor")
    early = max(lanes, width // 4)
    adv, down_grad, early_grad = down_grads(
        gst, place, slot_rows, score_rows, back, back_got, rows, up_got, early
    )
    early_got = partners(early_grad)

    base = base_parts(rows, weight, parts, (adv,))
    held = [base[i] for i in range(parts)]
    k = 1
    while 2 * k < parts:
        got = swap(jnp.stack(held[1::2]), k, "tensor")
        held = [
            (a.astype(f32) + got[i].astype(f32)).astype(bf) for i, a in enumerate(held[0::2])
        ]
        k *= 2
    zero_down = zeros((tasks, rank, width), (adv,))
    zero_up = zeros((tasks, rank, cols), (adv,))
    down_grad, base_mine, base_far, zero_down, zero_up = lax.optimization_barrier(
        (down_grad, held[0], held[1], zero_down, zero_up, *early_got)
    )[:5]
    base_got = swap(base_far, k, "tensor")
    down_grad_got = exchange(down_grad)

    ahead, ahead_wire = inner_down(slot_rows, rows, down_got, (base,))
    ahead, ahead_got = sum_first(ahead, ahead_wire, "tensor")
    inner_all, up_grad = up_grads(place, adv, ahead, ahead_got, cot, groups)
    up_grad_got = partners(up_grad)
    kv_new = adapted(place, inner_all, base_mine, base_got, up_got, (up_grad[0],))
    kv_out = kv_new.reshape(att, steps, cols)

    grad_down = combine(gst, trp, early_got, [down_grad_got], zero_down, (kv_new,))
    grad_up = combine(gst, trp, up_grad_got, [], zero_up, (grad_down,))
    return (kv_out, jnp.swapaxes(grad_down, 1, 2), grad_up)


def solution(mesh):
    in_specs = (
        P("dp", None, "tensor"),
        P("tensor", None),
        P("dp", "tensor", None),
        P("dp", None, "tensor"),
        P("dp", None),
        P(),
        P(),
        P("dp"),
        P("dp", None, "tensor"),
    )
    out_specs = (P("dp", None, "tensor"), P("dp", "tensor", None), P("dp", None, "tensor"))
    return jax.shard_map(body, mesh=mesh, in_specs=in_specs, out_specs=out_specs, check_vma=False)
```

```python
import functools

import jax
import jax.numpy as jnp
from jax import lax
from jax.experimental import pallas as pl
from jax.experimental.pallas import tpu as pltpu
from jax.sharding import PartitionSpec as P

scale = 0.25
bf = jnp.bfloat16
f32 = jnp.float32
big = 64 * 1024 * 1024
spare = 16
lanes = 128

ANY = pl.BlockSpec(memory_space=pl.ANY)
SMEM = pl.BlockSpec(memory_space=pltpu.SMEM)
VMEM = pl.BlockSpec(memory_space=pltpu.VMEM)


def shaped(shape, dtype):
    return jax.ShapeDtypeStruct(shape, dtype)


def call(kernel, outs, operands, specs, flops=0, scratch=(), after=(), vmem_outs=True):
    moved = sum(a.size * a.dtype.itemsize for a in list(operands) + list(outs))
    count = len(operands)

    def run(*refs):
        kernel(refs[:count], refs[count + len(after) :])

    return pl.pallas_call(
        run,
        out_shape=list(outs),
        in_specs=list(specs) + [ANY] * len(after),
        out_specs=[VMEM] * len(outs),
        scratch_shapes=list(scratch),
        compiler_params=pltpu.CompilerParams(vmem_limit_bytes=big),
        cost_estimate=pl.CostEstimate(flops=0, bytes_accessed=0, transcendentals=0),
    )(*operands, *after)


def swap(x, k, axis):
    n = lax.axis_size(axis)
    return lax.ppermute(x, axis, [(i, i ^ k) for i in range(n)])


def stored_row(gst, trp, tasks, k):
    me = lax.axis_index("dp")
    return lax.rem(trp[gst[me ^ k, me]], tasks)


def pack_up(gst, trp, up, slot_row, score_row):
    groups = gst.shape[0]
    tasks, rank, cols = up.shape
    tiles = cols // lanes

    def kernel(ins, outs):
        gst, trp, up, slot, score = ins
        sem = outs[-1]
        copies = []
        for k in reversed(range(groups)):
            row = stored_row(gst, trp, tasks, k)
            for j in range(tiles):
                copies.append(
                    pltpu.make_async_copy(
                        up.at[row, :, pl.ds(j * lanes, lanes)],
                        outs[k].at[pl.ds(j * rank, rank), :],
                        sem.at[k, j],
                    )
                )
                copies[-1].start()
        hot = slot[...] == lax.broadcasted_iota(jnp.int32, (groups, slot.shape[1]), 0)
        sums = jnp.sum(jnp.where(hot, score[...].astype(f32), 0.0), axis=1, keepdims=True)
        counts = jnp.sum(jnp.where(hot, 1.0, 0.0), axis=1, keepdims=True)
        here = lax.broadcasted_iota(jnp.int32, (groups, lanes), 0) == lax.broadcasted_iota(
            jnp.int32, (groups, lanes), 1
        )
        sums = jnp.sum(jnp.where(here, sums, 0.0), axis=0, keepdims=True)
        counts = jnp.sum(jnp.where(here, counts, 0.0), axis=0, keepdims=True)
        line = lax.broadcasted_iota(jnp.int32, (spare, lanes), 0)
        both = jnp.where(line == 0, sums, jnp.where(line == 1, counts, 0.0)).astype(bf)
        for k in range(groups):
            outs[k][tiles * rank :, :] = both
        for c in copies:
            c.wait()

    return call(
        kernel,
        [shaped((tiles * rank + spare, lanes), bf)] * groups,
        (gst, trp, up, slot_row, score_row),
        [SMEM, SMEM, ANY, VMEM, VMEM],
        scratch=[pltpu.SemaphoreType.DMA((groups, tiles))],
    )


def up_block(block, rank):
    tiles = block.shape[0] // rank
    return jnp.concatenate([block[j * rank : (j + 1) * rank, :] for j in range(tiles)], axis=1)


def pack_down(gst, trp, down, after):
    groups = gst.shape[0]
    tasks, rank, width = down.shape

    def kernel(ins, outs):
        gst, trp, down = ins
        out, sem = outs
        me = lax.axis_index("dp")
        copies = []
        for g in range(groups):
            row = lax.rem(trp[gst[g, me]], tasks)
            copies.append(pltpu.make_async_copy(down.at[row], out.at[g], sem.at[g]))
            copies[-1].start()
        for c in copies:
            c.wait()

    return call(
        kernel,
        [shaped((groups, rank, width), bf)],
        (gst, trp, down),
        [SMEM, SMEM, ANY],
        scratch=[pltpu.SemaphoreType.DMA((groups,))],
        after=after,
    )[0]


def base_parts(rows, weight, parts, shapes, after):
    n, width = rows.shape
    cols = weight.shape[1] // parts
    half = parts // 2
    tasks, rank = shapes[0][:2]
    widest = max(x[2] for x in shapes)
    mine = lax.axis_index("tensor").astype(jnp.int32).reshape(1)

    def shard(i, m):
        return m[0] ^ jnp.where(i < half, 2 * i + 1, 2 * (i - half))

    def kernel(mine, rows, weight, *rest):
        odd, even, *zeros, blank, sem = rest[len(after) :]
        step = pl.program_id(0)
        copies = [
            pltpu.make_async_copy(blank.at[:, pl.ds(0, z.shape[2])], z.at[t], sem.at[i, t])
            for i, z in enumerate(zeros)
            for t in range(tasks)
        ]

        @pl.when(step == 0)
        def _():
            blank[...] = jnp.zeros((rank, widest), bf)
            for c in copies:
                c.start()

        part = jnp.dot(rows[...], weight[...], preferred_element_type=f32).astype(bf)

        @pl.when(step < half)
        def _():
            odd[0] = part

        @pl.when(step >= half)
        def _():
            even[0] = part

        @pl.when(step == parts - 1)
        def _():
            for c in copies:
                c.wait()

    return pl.pallas_call(
        kernel,
        out_shape=[shaped((half, n, cols), bf)] * 2 + [shaped(x, bf) for x in shapes],
        grid_spec=pltpu.PrefetchScalarGridSpec(
            num_scalar_prefetch=1,
            grid=(parts,),
            in_specs=[
                pl.BlockSpec((n, width), lambda i, m: (0, 0)),
                pl.BlockSpec((width, cols), lambda i, m: (0, shard(i, m))),
            ]
            + [ANY] * len(after),
            out_specs=[
                pl.BlockSpec((1, n, cols), lambda i, m: (jnp.minimum(i, half - 1), 0, 0)),
                pl.BlockSpec((1, n, cols), lambda i, m: (jnp.maximum(i - half, 0), 0, 0)),
            ]
            + [ANY] * len(shapes),
            scratch_shapes=[
                pltpu.VMEM((rank, widest), bf),
                pltpu.SemaphoreType.DMA((len(shapes), tasks)),
            ],
        ),
        compiler_params=pltpu.CompilerParams(vmem_limit_bytes=big),
        cost_estimate=pl.CostEstimate(flops=0, bytes_accessed=0, transcendentals=0),
    )(mine, rows, weight, *after)


def inner_up(slot_row, score_row, rows, blocks, rank, after):
    n, cols = rows.shape
    att = slot_row.shape[1]
    steps = n // att

    def kernel(ins, outs):
        slot, score, rows = ins[:3]
        start = steps * lax.broadcasted_iota(jnp.int32, (att, n), 0)
        row = lax.broadcasted_iota(jnp.int32, (att, n), 1)
        own = jnp.logical_and(row >= start, row < start + steps).astype(bf)
        line = lax.broadcasted_iota(jnp.int32, (8, att), 0)
        both = jnp.where(line == 0, slot[...], jnp.where(line == 1, score[...], 0))
        both = jnp.dot(both.astype(f32).astype(bf), own, preferred_element_type=f32)
        slots = both[0:1, :].astype(jnp.int32)
        place = slots ^ lax.axis_index("dp")
        outs[2][...] = slots
        outs[3][...] = place
        outs[4][...] = both[1:2, :]
        wide = lax.dot_general(
            jnp.concatenate([up_block(block, rank) for block in ins[3:]], axis=0),
            rows[...],
            (((1,), (1,)), ((), ())),
            preferred_element_type=f32,
        )
        acc = jnp.zeros((rank, n), f32)
        for k in range(len(blocks)):
            acc = jnp.where(place == k, wide[k * rank : (k + 1) * rank], acc)
        outs[0][...] = acc
        outs[1][...] = acc.astype(bf)

    operands = (slot_row, score_row, rows, *blocks)
    return call(
        kernel,
        [shaped((rank, n), f32), shaped((rank, n), bf)]
        + [shaped((1, n), jnp.int32)] * 2
        + [shaped((1, n), f32)],
        operands,
        [VMEM] * len(operands),
        flops=2 * n * cols * rank * len(blocks),
        after=after,
    )


def inner_down(slot_rows, rows, blocks, after):
    groups, rank, width = blocks.shape
    n = rows.shape[0]

    def kernel(ins, outs):
        slot, rows, blocks = ins
        wide = lax.dot_general(
            blocks[...].reshape(groups * rank, width),
            rows[...],
            (((1,), (1,)), ((), ())),
            preferred_element_type=f32,
        )
        acc = jnp.zeros((rank, n), f32)
        for s in range(groups):
            acc = jnp.where(slot[...] == s, wide[s * rank : (s + 1) * rank], acc)
        outs[0][...] = acc
        outs[1][...] = acc.astype(bf)

    return call(
        kernel,
        [shaped((rank, n), f32), shaped((rank, n), bf)],
        (slot_rows, rows, blocks),
        [VMEM] * 3,
        flops=2 * n * width * rank * groups,
        after=after,
    )


def plus(x, got, after):
    def kernel(ins, outs):
        total = ins[0][...] + ins[1][...].astype(f32)
        outs[0][...] = total
        outs[1][...] = total.astype(bf)

    return call(kernel, [shaped(x.shape, f32), shaped(x.shape, bf)], (x, got), [VMEM] * 2, after=after)


def sum_first(x, wire, axis, after=()):
    k = 1
    while 2 * k < lax.axis_size(axis):
        x, wire = plus(x, swap(wire, k, axis), after)
        k *= 2
    return x, swap(wire, k, axis)


def spread(place, inner_t, k):
    return jnp.where(place == k, inner_t, jnp.zeros((), inner_t.dtype))


def down_grads(gst, place, slot_rows, score_rows, t, t_got, rows, up_blocks):
    groups = len(up_blocks)
    rank, n = t.shape
    width = rows.shape[1]

    def kernel(ins, outs):
        gst, place, slot, score, t, t_got, rows = ins[:7]
        me = lax.axis_index("dp")
        mine = gst[pl.ds(me, 1), :]
        sums = jnp.zeros((1, groups), f32)
        counts = jnp.zeros((1, groups), f32)
        for k, block in enumerate(ins[7:]):
            same = gst[pl.ds(me ^ k, 1), :] == mine
            x = block[block.shape[0] - spare :, :].astype(f32)
            sums += jnp.where(same, x[0:1, :groups], 0.0)
            counts += jnp.where(same, x[1:2, :groups], 0.0)
        mean = sums / jnp.maximum(counts, 1.0)
        here = lax.broadcasted_iota(jnp.int32, (groups, groups), 0) == lax.broadcasted_iota(
            jnp.int32, (groups, groups), 1
        )
        mean = jnp.sum(jnp.where(here, mean, 0.0), axis=1, keepdims=True)
        hot = slot[...] == lax.broadcasted_iota(jnp.int32, (groups, n), 0)
        adv = score[...] - jnp.sum(jnp.where(hot, mean, 0.0), axis=0, keepdims=True)
        total = (adv * (t[...] + t_got[...].astype(f32))).astype(bf)
        outs[0][...] = adv
        wide = jnp.concatenate([spread(place[...], total, k) for k in range(groups)], axis=0)
        chunk = width // 2 if width % 256 == 0 else width
        for first in range(0, width, chunk):
            part = jnp.dot(wide, rows[:, first : first + chunk], preferred_element_type=f32)
            part = (scale * part).astype(bf)
            for k in range(groups):
                outs[1 + k][:, first : first + chunk] = part[k * rank : (k + 1) * rank]

    operands = (gst, place, slot_rows, score_rows, t, t_got, rows, *up_blocks)
    out = call(
        kernel,
        [shaped((1, n), f32)] + [shaped((rank, width), bf)] * groups,
        operands,
        [VMEM] * len(operands),
        flops=2 * n * width * rank * groups,
    )
    return out[0], out[1:]


def up_grads(place, adv, t, t_got, cot, groups, after):
    rank, n = t.shape
    cols = cot.shape[1]

    def kernel(ins, outs):
        place, adv, t, t_got, cot = ins
        total = t[...] + t_got[...].astype(f32)
        total = (adv[...] * total).astype(bf)
        wide = jnp.concatenate([spread(place[...], total, k) for k in range(groups)], axis=0)
        part = (scale * jnp.dot(wide, cot[...], preferred_element_type=f32)).astype(bf)
        for k in range(groups):
            outs[k][...] = part[k * rank : (k + 1) * rank]

    return call(
        kernel,
        [shaped((rank, cols), bf)] * groups,
        (place, adv, t, t_got, cot),
        [VMEM] * 5,
        after=after,
        flops=2 * n * cols * rank * groups,
    )


def adapted(place, t, t_got, base_mine, base_got, blocks, after):
    n, cols = base_got.shape
    rank = t.shape[0]

    def kernel(ins, outs):
        place, t, t_got, base_mine, base_got = ins[:5]
        blocks = ins[5:]
        total = (t[...] + t_got[...].astype(f32)).astype(bf)
        wide = jnp.concatenate([spread(place[...], total, k) for k in range(len(blocks))], axis=0)
        ups = jnp.concatenate([up_block(b, rank) for b in blocks], axis=0)
        delta = lax.dot_general(wide, ups, (((0,), (0,)), ((), ())), preferred_element_type=f32)
        delta = (scale * delta).astype(bf).astype(f32)
        outs[0][...] = (base_mine[...].astype(f32) + base_got[...].astype(f32) + delta).astype(bf)

    operands = (place, t, t_got, base_mine, base_got, *blocks)
    return call(
        kernel,
        [shaped((n, cols), bf)],
        operands,
        [VMEM] * len(operands),
        flops=2 * n * cols * rank * len(blocks),
        after=after,
    )[0]


def combine(gst, trp, blocks, filled, after):
    groups = gst.shape[0]
    tasks, rank, width = filled.shape
    count = len(blocks)

    def kernel(*refs):
        gst, trp = refs[:2]
        ins = refs[2 : 2 + count]
        out, held, acc, sem_in, sem_out = refs[-5:]
        me = lax.axis_index("dp")
        copies = []
        for k in range(groups):
            source = ins[k] if count > 1 else ins[0].at[me ^ k]
            copies.append(pltpu.make_async_copy(source, held.at[k], sem_in.at[k]))
            copies[-1].start()
        rows = [stored_row(gst, trp, tasks, k) for k in range(groups)]
        back = [
            pltpu.make_async_copy(held.at[g], out.at[rows[g]], sem_out.at[g])
            for g in range(groups)
        ]
        last = []
        for g in range(groups):
            ends, again = jnp.bool_(True), jnp.bool_(False)
            for h in range(groups):
                if h > g:
                    ends = jnp.logical_and(ends, rows[h] != rows[g])
                if h < g:
                    again = jnp.logical_or(again, rows[h] == rows[g])
            last.append(ends)
            copies[g].wait()

            @pl.when(jnp.logical_and(ends, again))
            def _():
                acc[...] = held[g].astype(f32)
                for h in range(g):

                    @pl.when(rows[h] == rows[g])
                    def _():
                        acc[...] += held[h].astype(f32)

                held[g] = acc[...].astype(bf)

            @pl.when(ends)
            def _():
                back[g].start()

        for g in range(groups):

            @pl.when(last[g])
            def _():
                back[g].wait()

    return pl.pallas_call(
        kernel,
        out_shape=shaped(filled.shape, bf),
        in_specs=[SMEM, SMEM] + [ANY] * (count + 1 + len(after)),
        out_specs=ANY,
        scratch_shapes=[
            pltpu.VMEM((groups, rank, width), bf),
            pltpu.VMEM((rank, width), f32),
            pltpu.SemaphoreType.DMA((groups,)),
            pltpu.SemaphoreType.DMA((groups,)),
        ],
        input_output_aliases={2 + count: 0},
        compiler_params=pltpu.CompilerParams(vmem_limit_bytes=big),
        cost_estimate=pl.CostEstimate(flops=0, bytes_accessed=0, transcendentals=0),
    )(gst, trp, *blocks, filled, *after)


def exchange(x):
    return lax.all_to_all(x, "dp", split_axis=0, concat_axis=0, tiled=True)


def partners(blocks):
    got = {k: swap(blocks[k], k, "dp") for k in reversed(range(1, len(blocks)))}
    return [blocks[0]] + [got[k] for k in range(1, len(blocks))]


def body(hidden, weight, down, up, slot, gst, trp, scores, cotangent):
    groups, parts = lax.axis_size("dp"), lax.axis_size("tensor")
    half = groups // 2
    me = lax.axis_index("dp")
    att, steps, width = hidden.shape
    cols = cotangent.shape[2]
    n = att * steps
    tasks, rank = down.shape[0], down.shape[2]
    down = jnp.swapaxes(down, 1, 2)

    slot_row = slot.reshape(1, att)
    score_row = scores.reshape(1, att)
    up_out = pack_up(gst, trp, up, slot_row, score_row)
    up_got = partners(up_out)
    down_out = pack_down(gst, trp, down, (up_out[0],))
    down_got = exchange(lax.optimization_barrier((down_out, *up_got))[0])

    hidden, cotangent, _ = lax.optimization_barrier((hidden, cotangent, up_out[0]))
    cot = cotangent.reshape(n, cols)
    rows = hidden.reshape(n, width)

    back, back_wire, slot_rows, place, score_rows = inner_up(
        slot_row, score_row, cot, up_got, rank, ()
    )
    back, back_got = sum_first(back, back_wire, "tensor")
    adv, down_grad = down_grads(
        gst, place, slot_rows, score_rows, back, back_got, rows, up_got
    )
    late = range(half + half // 2, groups)
    down_grad = list(down_grad)
    for k in late:
        down_grad[k] = lax.optimization_barrier((down_grad[k], down_got))[0]
    down_grad_got = partners(down_grad)

    odd, even, zero_down, zero_up = base_parts(
        rows, weight, parts, ((tasks, rank, width), (tasks, rank, cols)), (adv,)
    )
    held, k = [odd, even], 1
    while 2 * k < parts:
        got = swap(held[0], k, "tensor").astype(f32)
        both = (held[1].astype(f32) + got).astype(bf)
        held, k = [both[1::2], both[0::2]], 2 * k
    base_far, base_mine = held[0].reshape(n, cols), held[1].reshape(n, cols)
    base_got = swap(base_far, k, "tensor")

    ahead, ahead_wire = inner_down(slot_rows, rows, down_got, (base_got, *down_grad_got[1:half]))
    ahead, ahead_got = sum_first(ahead, ahead_wire, "tensor")
    kv_new = adapted(place, ahead, ahead_got, base_mine, base_got, up_got, ())
    kv_out = kv_new.reshape(att, steps, cols)
    up_grad = up_grads(
        place, adv, ahead, ahead_got, cot, groups, (kv_out, *down_grad_got[half : half + half // 2])
    )
    up_grad_got = [up_grad[0]] + [None] * (groups - 1)
    for k in [*range(half, groups), *range(1, half)]:
        x = lax.optimization_barrier((up_grad[k], down_grad_got[k]))[0]
        up_grad_got[k] = swap(x, k, "dp")
    grad_down = combine(gst, trp, down_grad_got, zero_down, ())
    grad_up = combine(gst, trp, up_grad_got, zero_up, (grad_down,))
    return (kv_out, jnp.swapaxes(grad_down, 1, 2), grad_up)


def solution(mesh):
    in_specs = (
        P("dp", None, "tensor"),
        P("tensor", None),
        P("dp", "tensor", None),
        P("dp", None, "tensor"),
        P("dp", None),
        P(),
        P(),
        P("dp"),
        P("dp", None, "tensor"),
    )
    out_specs = (P("dp", None, "tensor"), P("dp", "tensor", None), P("dp", None, "tensor"))
    return jax.shard_map(body, mesh=mesh, in_specs=in_specs, out_specs=out_specs, check_vma=False)
```

```python
import functools

import jax
import jax.numpy as jnp
from jax import lax
from jax.experimental import pallas as pl
from jax.experimental.pallas import tpu as pltpu
from jax.sharding import PartitionSpec as P

scale = 0.25
bf = jnp.bfloat16
f32 = jnp.float32
big = 64 * 1024 * 1024
spare = 16
lanes = 128

ANY = pl.BlockSpec(memory_space=pl.ANY)
SMEM = pl.BlockSpec(memory_space=pltpu.SMEM)
VMEM = pl.BlockSpec(memory_space=pltpu.VMEM)


def shaped(shape, dtype):
    return jax.ShapeDtypeStruct(shape, dtype)


def call(kernel, outs, operands, specs, flops=0, scratch=(), after=(), vmem_outs=True):
    moved = sum(a.size * a.dtype.itemsize for a in list(operands) + list(outs))
    count = len(operands)

    def run(*refs):
        kernel(refs[:count], refs[count + len(after) :])

    return pl.pallas_call(
        run,
        out_shape=list(outs),
        in_specs=list(specs) + [ANY] * len(after),
        out_specs=[VMEM] * len(outs),
        scratch_shapes=list(scratch),
        compiler_params=pltpu.CompilerParams(vmem_limit_bytes=big),
        cost_estimate=pl.CostEstimate(flops=0, bytes_accessed=0, transcendentals=0),
    )(*operands, *after)


def swap(x, k, axis):
    n = lax.axis_size(axis)
    return lax.ppermute(x, axis, [(i, i ^ k) for i in range(n)])


def stored_row(gst, trp, tasks, k):
    me = lax.axis_index("dp")
    return lax.rem(trp[gst[me ^ k, me]], tasks)


def pack_up(gst, trp, up, slot_row, score_row):
    groups = gst.shape[0]
    tasks, rank, cols = up.shape
    tiles = cols // lanes

    def kernel(ins, outs):
        gst, trp, up, slot, score = ins
        sem = outs[-1]
        copies = []
        for k in reversed(range(groups)):
            row = stored_row(gst, trp, tasks, k)
            for j in range(tiles):
                copies.append(
                    pltpu.make_async_copy(
                        up.at[row, :, pl.ds(j * lanes, lanes)],
                        outs[k].at[pl.ds(j * rank, rank), :],
                        sem.at[k, j],
                    )
                )
                copies[-1].start()
        hot = slot[...] == lax.broadcasted_iota(jnp.int32, (groups, slot.shape[1]), 0)
        sums = jnp.sum(jnp.where(hot, score[...].astype(f32), 0.0), axis=1, keepdims=True)
        counts = jnp.sum(jnp.where(hot, 1.0, 0.0), axis=1, keepdims=True)
        here = lax.broadcasted_iota(jnp.int32, (groups, lanes), 0) == lax.broadcasted_iota(
            jnp.int32, (groups, lanes), 1
        )
        sums = jnp.sum(jnp.where(here, sums, 0.0), axis=0, keepdims=True)
        counts = jnp.sum(jnp.where(here, counts, 0.0), axis=0, keepdims=True)
        line = lax.broadcasted_iota(jnp.int32, (spare, lanes), 0)
        both = jnp.where(line == 0, sums, jnp.where(line == 1, counts, 0.0)).astype(bf)
        for k in range(groups):
            outs[k][tiles * rank :, :] = both
        for c in copies:
            c.wait()

    return call(
        kernel,
        [shaped((tiles * rank + spare, lanes), bf)] * groups,
        (gst, trp, up, slot_row, score_row),
        [SMEM, SMEM, ANY, VMEM, VMEM],
        scratch=[pltpu.SemaphoreType.DMA((groups, tiles))],
    )


def up_block(block, rank):
    tiles = block.shape[0] // rank
    return jnp.concatenate([block[j * rank : (j + 1) * rank, :] for j in range(tiles)], axis=1)


def pack_down(gst, trp, down, after):
    groups = gst.shape[0]
    tasks, rank, width = down.shape

    def kernel(ins, outs):
        gst, trp, down = ins
        out, sem = outs
        me = lax.axis_index("dp")
        copies = []
        for g in range(groups):
            row = lax.rem(trp[gst[g, me]], tasks)
            copies.append(pltpu.make_async_copy(down.at[row], out.at[g], sem.at[g]))
            copies[-1].start()
        for c in copies:
            c.wait()

    return call(
        kernel,
        [shaped((groups, rank, width), bf)],
        (gst, trp, down),
        [SMEM, SMEM, ANY],
        scratch=[pltpu.SemaphoreType.DMA((groups,))],
        after=after,
    )[0]


def base_parts(rows, weight, parts, shapes, after):
    n, width = rows.shape
    cols = weight.shape[1] // parts
    half = parts // 2
    tasks, rank = shapes[0][:2]
    widest = max(x[2] for x in shapes)
    mine = lax.axis_index("tensor").astype(jnp.int32).reshape(1)

    def shard(i, m):
        return m[0] ^ jnp.where(i < half, 2 * i + 1, 2 * (i - half))

    def kernel(mine, rows, weight, *rest):
        odd, even, *zeros, blank, sem = rest[len(after) :]
        step = pl.program_id(0)
        copies = [
            pltpu.make_async_copy(blank.at[:, pl.ds(0, z.shape[2])], z.at[t], sem.at[i, t])
            for i, z in enumerate(zeros)
            for t in range(tasks)
        ]

        @pl.when(step == 0)
        def _():
            blank[...] = jnp.zeros((rank, widest), bf)
            for c in copies:
                c.start()

        part = jnp.dot(rows[...], weight[...], preferred_element_type=f32).astype(bf)

        @pl.when(step < half)
        def _():
            odd[0] = part

        @pl.when(step >= half)
        def _():
            even[0] = part

        @pl.when(step == parts - 1)
        def _():
            for c in copies:
                c.wait()

    return pl.pallas_call(
        kernel,
        out_shape=[shaped((half, n, cols), bf)] * 2 + [shaped(x, bf) for x in shapes],
        grid_spec=pltpu.PrefetchScalarGridSpec(
            num_scalar_prefetch=1,
            grid=(parts,),
            in_specs=[
                pl.BlockSpec((n, width), lambda i, m: (0, 0)),
                pl.BlockSpec((width, cols), lambda i, m: (0, shard(i, m))),
            ]
            + [ANY] * len(after),
            out_specs=[
                pl.BlockSpec((1, n, cols), lambda i, m: (jnp.minimum(i, half - 1), 0, 0)),
                pl.BlockSpec((1, n, cols), lambda i, m: (jnp.maximum(i - half, 0), 0, 0)),
            ]
            + [ANY] * len(shapes),
            scratch_shapes=[
                pltpu.VMEM((rank, widest), bf),
                pltpu.SemaphoreType.DMA((len(shapes), tasks)),
            ],
        ),
        compiler_params=pltpu.CompilerParams(vmem_limit_bytes=big),
        cost_estimate=pl.CostEstimate(flops=0, bytes_accessed=0, transcendentals=0),
    )(mine, rows, weight, *after)


def inner_up(slot_row, score_row, rows, blocks, rank, after):
    n, cols = rows.shape
    att = slot_row.shape[1]
    steps = n // att

    def kernel(ins, outs):
        slot, score, rows = ins[:3]
        start = steps * lax.broadcasted_iota(jnp.int32, (att, n), 0)
        row = lax.broadcasted_iota(jnp.int32, (att, n), 1)
        own = jnp.logical_and(row >= start, row < start + steps).astype(bf)
        line = lax.broadcasted_iota(jnp.int32, (8, att), 0)
        both = jnp.where(line == 0, slot[...], jnp.where(line == 1, score[...], 0))
        both = jnp.dot(both.astype(f32).astype(bf), own, preferred_element_type=f32)
        slots = both[0:1, :].astype(jnp.int32)
        place = slots ^ lax.axis_index("dp")
        outs[2][...] = slots
        outs[3][...] = place
        outs[4][...] = both[1:2, :]
        wide = lax.dot_general(
            jnp.concatenate([up_block(block, rank) for block in ins[3:]], axis=0),
            rows[...],
            (((1,), (1,)), ((), ())),
            preferred_element_type=f32,
        )
        acc = jnp.zeros((rank, n), f32)
        for k in range(len(blocks)):
            acc = jnp.where(place == k, wide[k * rank : (k + 1) * rank], acc)
        outs[0][...] = acc
        outs[1][...] = acc.astype(bf)

    operands = (slot_row, score_row, rows, *blocks)
    return call(
        kernel,
        [shaped((rank, n), f32), shaped((rank, n), bf)]
        + [shaped((1, n), jnp.int32)] * 2
        + [shaped((1, n), f32)],
        operands,
        [VMEM] * len(operands),
        flops=2 * n * cols * rank * len(blocks),
        after=after,
    )


def inner_down(slot_rows, rows, blocks, after):
    groups, rank, width = blocks.shape
    n = rows.shape[0]

    def kernel(ins, outs):
        slot, rows, blocks = ins
        wide = lax.dot_general(
            blocks[...].reshape(groups * rank, width),
            rows[...],
            (((1,), (1,)), ((), ())),
            preferred_element_type=f32,
        )
        acc = jnp.zeros((rank, n), f32)
        for s in range(groups):
            acc = jnp.where(slot[...] == s, wide[s * rank : (s + 1) * rank], acc)
        outs[0][...] = acc
        outs[1][...] = acc.astype(bf)

    return call(
        kernel,
        [shaped((rank, n), f32), shaped((rank, n), bf)],
        (slot_rows, rows, blocks),
        [VMEM] * 3,
        flops=2 * n * width * rank * groups,
        after=after,
    )


def plus(x, got, after):
    def kernel(ins, outs):
        total = ins[0][...] + ins[1][...].astype(f32)
        outs[0][...] = total
        outs[1][...] = total.astype(bf)

    return call(kernel, [shaped(x.shape, f32), shaped(x.shape, bf)], (x, got), [VMEM] * 2, after=after)


def sum_first(x, wire, axis, after=()):
    k = 1
    while 2 * k < lax.axis_size(axis):
        x, wire = plus(x, swap(wire, k, axis), after)
        k *= 2
    return x, swap(wire, k, axis)


def spread(place, inner_t, k):
    return jnp.where(place == k, inner_t, jnp.zeros((), inner_t.dtype))


def down_grads(gst, place, slot_rows, score_rows, t, t_got, rows, up_blocks):
    groups = len(up_blocks)
    rank, n = t.shape
    width = rows.shape[1]

    def kernel(ins, outs):
        gst, place, slot, score, t, t_got, rows = ins[:7]
        me = lax.axis_index("dp")
        mine = gst[pl.ds(me, 1), :]
        sums = jnp.zeros((1, groups), f32)
        counts = jnp.zeros((1, groups), f32)
        for k, block in enumerate(ins[7:]):
            same = gst[pl.ds(me ^ k, 1), :] == mine
            x = block[block.shape[0] - spare :, :].astype(f32)
            sums += jnp.where(same, x[0:1, :groups], 0.0)
            counts += jnp.where(same, x[1:2, :groups], 0.0)
        mean = sums / jnp.maximum(counts, 1.0)
        here = lax.broadcasted_iota(jnp.int32, (groups, groups), 0) == lax.broadcasted_iota(
            jnp.int32, (groups, groups), 1
        )
        mean = jnp.sum(jnp.where(here, mean, 0.0), axis=1, keepdims=True)
        hot = slot[...] == lax.broadcasted_iota(jnp.int32, (groups, n), 0)
        adv = score[...] - jnp.sum(jnp.where(hot, mean, 0.0), axis=0, keepdims=True)
        total = (adv * (t[...] + t_got[...].astype(f32))).astype(bf)
        outs[0][...] = adv
        wide = jnp.concatenate([spread(place[...], total, k) for k in range(groups)], axis=0)
        chunk = width // 2 if width % 256 == 0 else width
        for first in range(0, width, chunk):
            part = jnp.dot(wide, rows[:, first : first + chunk], preferred_element_type=f32)
            part = (scale * part).astype(bf)
            for k in range(groups):
                outs[1 + k][:, first : first + chunk] = part[k * rank : (k + 1) * rank]

    operands = (gst, place, slot_rows, score_rows, t, t_got, rows, *up_blocks)
    out = call(
        kernel,
        [shaped((1, n), f32)] + [shaped((rank, width), bf)] * groups,
        operands,
        [VMEM] * len(operands),
        flops=2 * n * width * rank * groups,
    )
    return out[0], out[1:]


def up_grads(place, adv, t, t_got, cot, groups, after):
    rank, n = t.shape
    cols = cot.shape[1]

    def kernel(ins, outs):
        place, adv, t, t_got, cot = ins
        total = t[...] + t_got[...].astype(f32)
        total = (adv[...] * total).astype(bf)
        wide = jnp.concatenate([spread(place[...], total, k) for k in range(groups)], axis=0)
        part = (scale * jnp.dot(wide, cot[...], preferred_element_type=f32)).astype(bf)
        for k in range(groups):
            outs[k][...] = part[k * rank : (k + 1) * rank]

    return call(
        kernel,
        [shaped((rank, cols), bf)] * groups,
        (place, adv, t, t_got, cot),
        [VMEM] * 5,
        after=after,
        flops=2 * n * cols * rank * groups,
    )


def adapted(place, t, t_got, base_mine, base_got, blocks, after):
    n, cols = base_got.shape
    rank = t.shape[0]

    def kernel(ins, outs):
        place, t, t_got, base_mine, base_got = ins[:5]
        blocks = ins[5:]
        total = (t[...] + t_got[...].astype(f32)).astype(bf)
        wide = jnp.concatenate([spread(place[...], total, k) for k in range(len(blocks))], axis=0)
        ups = jnp.concatenate([up_block(b, rank) for b in blocks], axis=0)
        delta = lax.dot_general(wide, ups, (((0,), (0,)), ((), ())), preferred_element_type=f32)
        delta = (scale * delta).astype(bf).astype(f32)
        outs[0][...] = (base_mine[...].astype(f32) + base_got[...].astype(f32) + delta).astype(bf)

    operands = (place, t, t_got, base_mine, base_got, *blocks)
    return call(
        kernel,
        [shaped((n, cols), bf)],
        operands,
        [VMEM] * len(operands),
        flops=2 * n * cols * rank * len(blocks),
        after=after,
    )[0]


def combine(gst, trp, blocks, filled, after):
    groups = gst.shape[0]
    tasks, rank, width = filled.shape
    count = len(blocks)

    def kernel(*refs):
        tables = refs[:2]
        ins = refs[2 : 2 + count]
        out, held, acc, gst, trp, sem_in, sem_out, sem = refs[-8:]
        loads = [pltpu.make_async_copy(a, b, sem.at[i]) for i, (a, b) in enumerate(zip(tables, (gst, trp)))]
        for c in loads:
            c.start()
        me = lax.axis_index("dp")
        copies = []
        for k in range(groups):
            source = ins[k] if count > 1 else ins[0].at[me ^ k]
            copies.append(pltpu.make_async_copy(source, held.at[k], sem_in.at[k]))
            copies[-1].start()
        for c in loads:
            c.wait()
        rows = [stored_row(gst, trp, tasks, k) for k in range(groups)]
        back = [
            pltpu.make_async_copy(held.at[g], out.at[rows[g]], sem_out.at[g])
            for g in range(groups)
        ]
        last = []
        for g in range(groups):
            ends, again = jnp.bool_(True), jnp.bool_(False)
            for h in range(groups):
                if h > g:
                    ends = jnp.logical_and(ends, rows[h] != rows[g])
                if h < g:
                    again = jnp.logical_or(again, rows[h] == rows[g])
            last.append(ends)
            copies[g].wait()

            @pl.when(jnp.logical_and(ends, again))
            def _():
                acc[...] = held[g].astype(f32)
                for h in range(g):

                    @pl.when(rows[h] == rows[g])
                    def _():
                        acc[...] += held[h].astype(f32)

                held[g] = acc[...].astype(bf)

            @pl.when(ends)
            def _():
                back[g].start()

        for g in range(groups):

            @pl.when(last[g])
            def _():
                back[g].wait()

    return pl.pallas_call(
        kernel,
        out_shape=shaped(filled.shape, bf),
        in_specs=[ANY] * (count + 3 + len(after)),
        out_specs=ANY,
        scratch_shapes=[
            pltpu.VMEM((groups, rank, width), bf),
            pltpu.VMEM((rank, width), f32),
            pltpu.SMEM(gst.shape, jnp.int32),
            pltpu.SMEM(trp.shape, jnp.int32),
            pltpu.SemaphoreType.DMA((groups,)),
            pltpu.SemaphoreType.DMA((groups,)),
            pltpu.SemaphoreType.DMA((2,)),
        ],
        input_output_aliases={2 + count: 0},
        compiler_params=pltpu.CompilerParams(vmem_limit_bytes=big),
        cost_estimate=pl.CostEstimate(flops=0, bytes_accessed=0, transcendentals=0),
    )(gst, trp, *blocks, filled, *after)


def exchange(x):
    return lax.all_to_all(x, "dp", split_axis=0, concat_axis=0, tiled=True)


def partners(blocks):
    got = {k: swap(blocks[k], k, "dp") for k in reversed(range(1, len(blocks)))}
    return [blocks[0]] + [got[k] for k in range(1, len(blocks))]


def body(hidden, weight, down, up, slot, gst, trp, scores, cotangent):
    groups, parts = lax.axis_size("dp"), lax.axis_size("tensor")
    half = groups // 2
    me = lax.axis_index("dp")
    att, steps, width = hidden.shape
    cols = cotangent.shape[2]
    n = att * steps
    tasks, rank = down.shape[0], down.shape[2]
    down = jnp.swapaxes(down, 1, 2)

    slot_row = slot.reshape(1, att)
    score_row = scores.reshape(1, att)
    up_out = pack_up(gst, trp, up, slot_row, score_row)
    up_got = partners(up_out)
    down_out = pack_down(gst, trp, down, (up_out[0],))
    down_got = exchange(lax.optimization_barrier((down_out, *up_got))[0])

    hidden, cotangent, _ = lax.optimization_barrier((hidden, cotangent, up_out[0]))
    cot = cotangent.reshape(n, cols)
    rows = hidden.reshape(n, width)

    back, back_wire, slot_rows, place, score_rows = inner_up(
        slot_row, score_row, cot, up_got, rank, ()
    )
    back, back_got = sum_first(back, back_wire, "tensor")
    adv, down_grad = down_grads(
        gst, place, slot_rows, score_rows, back, back_got, rows, up_got
    )
    late = range(half + half // 2, groups)
    down_grad = list(down_grad)
    for k in late:
        down_grad[k] = lax.optimization_barrier((down_grad[k], down_got))[0]
    down_grad_got = partners(down_grad)

    odd, even, zero_down, zero_up = base_parts(
        rows, weight, parts, ((tasks, rank, width), (tasks, rank, cols)), (adv,)
    )
    held, k = [odd, even], 1
    while 2 * k < parts:
        got = swap(held[0], k, "tensor").astype(f32)
        both = (held[1].astype(f32) + got).astype(bf)
        held, k = [both[1::2], both[0::2]], 2 * k
    base_far, base_mine = held[0].reshape(n, cols), held[1].reshape(n, cols)
    base_got = swap(base_far, k, "tensor")

    ahead, ahead_wire = inner_down(slot_rows, rows, down_got, (base_got, *down_grad_got[1:half]))
    ahead, ahead_got = sum_first(ahead, ahead_wire, "tensor")
    kv_new = adapted(place, ahead, ahead_got, base_mine, base_got, up_got, ())
    kv_out = kv_new.reshape(att, steps, cols)
    up_grad = up_grads(
        place, adv, ahead, ahead_got, cot, groups, (kv_out, *down_grad_got[half : half + half // 2])
    )
    up_grad_got = [up_grad[0]] + [None] * (groups - 1)
    for k in [*range(half, groups), *range(1, half)]:
        x = lax.optimization_barrier((up_grad[k], down_grad_got[k]))[0]
        up_grad_got[k] = swap(x, k, "dp")
    grad_down = combine(gst, trp, down_grad_got, zero_down, ())
    grad_up = combine(gst, trp, up_grad_got, zero_up, (grad_down,))
    return (kv_out, jnp.swapaxes(grad_down, 1, 2), grad_up)


def solution(mesh):
    in_specs = (
        P("dp", None, "tensor"),
        P("tensor", None),
        P("dp", "tensor", None),
        P("dp", None, "tensor"),
        P("dp", None),
        P(),
        P(),
        P("dp"),
        P("dp", None, "tensor"),
    )
    out_specs = (P("dp", None, "tensor"), P("dp", "tensor", None), P("dp", None, "tensor"))
    return jax.shard_map(body, mesh=mesh, in_specs=in_specs, out_specs=out_specs, check_vma=False)
```

```python
import functools

import jax
import jax.numpy as jnp
from jax import lax
from jax.experimental import pallas as pl
from jax.experimental.pallas import tpu as pltpu
from jax.sharding import PartitionSpec as P

scale = 0.25
bf = jnp.bfloat16
f32 = jnp.float32
big = 64 * 1024 * 1024
spare = 16
lanes = 128

ANY = pl.BlockSpec(memory_space=pl.ANY)
SMEM = pl.BlockSpec(memory_space=pltpu.SMEM)
VMEM = pl.BlockSpec(memory_space=pltpu.VMEM)


def shaped(shape, dtype):
    return jax.ShapeDtypeStruct(shape, dtype)


def call(kernel, outs, operands, specs, flops=0, scratch=(), after=(), vmem_outs=True):
    moved = sum(a.size * a.dtype.itemsize for a in list(operands) + list(outs))
    count = len(operands)

    def run(*refs):
        kernel(refs[:count], refs[count + len(after) :])

    return pl.pallas_call(
        run,
        out_shape=list(outs),
        in_specs=list(specs) + [ANY] * len(after),
        out_specs=[VMEM] * len(outs),
        scratch_shapes=list(scratch),
        compiler_params=pltpu.CompilerParams(vmem_limit_bytes=big),
        cost_estimate=pl.CostEstimate(flops=0, bytes_accessed=0, transcendentals=0),
    )(*operands, *after)


def swap(x, k, axis):
    n = lax.axis_size(axis)
    return lax.ppermute(x, axis, [(i, i ^ k) for i in range(n)])


def stored_row(gst, trp, tasks, k):
    me = lax.axis_index("dp")
    return lax.rem(trp[gst[me ^ k, me]], tasks)


def pack_up(gst, trp, up, slot_row, score_row):
    groups = gst.shape[0]
    tasks, rank, cols = up.shape
    tiles = cols // lanes

    def kernel(ins, outs):
        gst, trp, up, slot, score = ins
        sem = outs[-1]
        copies = []
        for k in reversed(range(groups)):
            row = stored_row(gst, trp, tasks, k)
            for j in range(tiles):
                copies.append(
                    pltpu.make_async_copy(
                        up.at[row, :, pl.ds(j * lanes, lanes)],
                        outs[k].at[pl.ds(j * rank, rank), :],
                        sem.at[k, j],
                    )
                )
                copies[-1].start()
        hot = slot[...] == lax.broadcasted_iota(jnp.int32, (groups, slot.shape[1]), 0)
        sums = jnp.sum(jnp.where(hot, score[...].astype(f32), 0.0), axis=1, keepdims=True)
        counts = jnp.sum(jnp.where(hot, 1.0, 0.0), axis=1, keepdims=True)
        here = lax.broadcasted_iota(jnp.int32, (groups, lanes), 0) == lax.broadcasted_iota(
            jnp.int32, (groups, lanes), 1
        )
        sums = jnp.sum(jnp.where(here, sums, 0.0), axis=0, keepdims=True)
        counts = jnp.sum(jnp.where(here, counts, 0.0), axis=0, keepdims=True)
        line = lax.broadcasted_iota(jnp.int32, (spare, lanes), 0)
        both = jnp.where(line == 0, sums, jnp.where(line == 1, counts, 0.0)).astype(bf)
        for k in range(groups):
            outs[k][tiles * rank :, :] = both
        for c in copies:
            c.wait()

    return call(
        kernel,
        [shaped((tiles * rank + spare, lanes), bf)] * groups,
        (gst, trp, up, slot_row, score_row),
        [SMEM, SMEM, ANY, VMEM, VMEM],
        scratch=[pltpu.SemaphoreType.DMA((groups, tiles))],
    )


def up_block(block, rank):
    tiles = block.shape[0] // rank
    return jnp.concatenate([block[j * rank : (j + 1) * rank, :] for j in range(tiles)], axis=1)


def pack_down(gst, trp, down, after):
    groups = gst.shape[0]
    tasks, rank, width = down.shape

    def kernel(ins, outs):
        gst, trp, down = ins
        out, sem = outs
        me = lax.axis_index("dp")
        copies = []
        for g in range(groups):
            row = lax.rem(trp[gst[g, me]], tasks)
            copies.append(pltpu.make_async_copy(down.at[row], out.at[g], sem.at[g]))
            copies[-1].start()
        for c in copies:
            c.wait()

    return call(
        kernel,
        [shaped((groups, rank, width), bf)],
        (gst, trp, down),
        [SMEM, SMEM, ANY],
        scratch=[pltpu.SemaphoreType.DMA((groups,))],
        after=after,
    )[0]


def base_parts(rows, weight, parts, shapes, after):
    n, width = rows.shape
    cols = weight.shape[1] // parts
    half = parts // 2
    tasks, rank = shapes[0][:2]
    widest = max(x[2] for x in shapes)
    mine = lax.axis_index("tensor").astype(jnp.int32).reshape(1)

    def shard(i, m):
        return m[0] ^ jnp.where(i < half, 2 * i + 1, 2 * (i - half))

    def kernel(mine, rows, weight, *rest):
        odd, even, *zeros, blank, sem = rest[len(after) :]
        step = pl.program_id(0)
        copies = [
            pltpu.make_async_copy(blank.at[:, pl.ds(0, z.shape[2])], z.at[t], sem.at[i, t])
            for i, z in enumerate(zeros)
            for t in range(tasks)
        ]

        @pl.when(step == 0)
        def _():
            blank[...] = jnp.zeros((rank, widest), bf)
            for c in copies:
                c.start()

        part = jnp.dot(rows[...], weight[...], preferred_element_type=f32).astype(bf)

        @pl.when(step < half)
        def _():
            odd[0] = part

        @pl.when(step >= half)
        def _():
            even[0] = part

        @pl.when(step == parts - 1)
        def _():
            for c in copies:
                c.wait()

    return pl.pallas_call(
        kernel,
        out_shape=[shaped((half, n, cols), bf)] * 2 + [shaped(x, bf) for x in shapes],
        grid_spec=pltpu.PrefetchScalarGridSpec(
            num_scalar_prefetch=1,
            grid=(parts,),
            in_specs=[
                pl.BlockSpec((n, width), lambda i, m: (0, 0)),
                pl.BlockSpec((width, cols), lambda i, m: (0, shard(i, m))),
            ]
            + [ANY] * len(after),
            out_specs=[
                pl.BlockSpec((1, n, cols), lambda i, m: (jnp.minimum(i, half - 1), 0, 0)),
                pl.BlockSpec((1, n, cols), lambda i, m: (jnp.maximum(i - half, 0), 0, 0)),
            ]
            + [ANY] * len(shapes),
            scratch_shapes=[
                pltpu.VMEM((rank, widest), bf),
                pltpu.SemaphoreType.DMA((len(shapes), tasks)),
            ],
        ),
        compiler_params=pltpu.CompilerParams(vmem_limit_bytes=big),
        cost_estimate=pl.CostEstimate(flops=0, bytes_accessed=0, transcendentals=0),
    )(mine, rows, weight, *after)


def inner_up(slot_row, score_row, rows, blocks, rank, after):
    n, cols = rows.shape
    att = slot_row.shape[1]
    steps = n // att

    def kernel(ins, outs):
        slot, score, rows = ins[:3]
        start = steps * lax.broadcasted_iota(jnp.int32, (att, n), 0)
        row = lax.broadcasted_iota(jnp.int32, (att, n), 1)
        own = jnp.logical_and(row >= start, row < start + steps).astype(bf)
        line = lax.broadcasted_iota(jnp.int32, (8, att), 0)
        both = jnp.where(line == 0, slot[...], jnp.where(line == 1, score[...], 0))
        both = jnp.dot(both.astype(f32).astype(bf), own, preferred_element_type=f32)
        slots = both[0:1, :].astype(jnp.int32)
        place = slots ^ lax.axis_index("dp")
        outs[2][...] = slots
        outs[3][...] = place
        outs[4][...] = both[1:2, :]
        wide = lax.dot_general(
            jnp.concatenate([up_block(block, rank) for block in ins[3:]], axis=0),
            rows[...],
            (((1,), (1,)), ((), ())),
            preferred_element_type=f32,
        )
        acc = jnp.zeros((rank, n), f32)
        for k in range(len(blocks)):
            acc = jnp.where(place == k, wide[k * rank : (k + 1) * rank], acc)
        outs[0][...] = acc
        outs[1][...] = acc.astype(bf)

    operands = (slot_row, score_row, rows, *blocks)
    return call(
        kernel,
        [shaped((rank, n), f32), shaped((rank, n), bf)]
        + [shaped((1, n), jnp.int32)] * 2
        + [shaped((1, n), f32)],
        operands,
        [VMEM] * len(operands),
        flops=2 * n * cols * rank * len(blocks),
        after=after,
    )


def inner_down(slot_rows, rows, blocks, after):
    groups, rank, width = blocks.shape
    n = rows.shape[0]

    def kernel(ins, outs):
        slot, rows, blocks = ins
        wide = lax.dot_general(
            blocks[...].reshape(groups * rank, width),
            rows[...],
            (((1,), (1,)), ((), ())),
            preferred_element_type=f32,
        )
        acc = jnp.zeros((rank, n), f32)
        for s in range(groups):
            acc = jnp.where(slot[...] == s, wide[s * rank : (s + 1) * rank], acc)
        outs[0][...] = acc
        outs[1][...] = acc.astype(bf)

    return call(
        kernel,
        [shaped((rank, n), f32), shaped((rank, n), bf)],
        (slot_rows, rows, blocks),
        [VMEM] * 3,
        flops=2 * n * width * rank * groups,
        after=after,
    )


def plus(x, got, after):
    def kernel(ins, outs):
        total = ins[0][...] + ins[1][...].astype(f32)
        outs[0][...] = total
        outs[1][...] = total.astype(bf)

    return call(kernel, [shaped(x.shape, f32), shaped(x.shape, bf)], (x, got), [VMEM] * 2, after=after)


def sum_first(x, wire, axis, after=()):
    k = 1
    while 2 * k < lax.axis_size(axis):
        x, wire = plus(x, swap(wire, k, axis), after)
        k *= 2
    return x, swap(wire, k, axis)


def spread(place, inner_t, k):
    return jnp.where(place == k, inner_t, jnp.zeros((), inner_t.dtype))


def down_grads(gst, place, slot_rows, score_rows, t, t_got, rows, up_blocks):
    groups = len(up_blocks)
    rank, n = t.shape
    width = rows.shape[1]

    def kernel(ins, outs):
        gst, place, slot, score, t, t_got, rows = ins[:7]
        me = lax.axis_index("dp")
        mine = gst[pl.ds(me, 1), :]
        sums = jnp.zeros((1, groups), f32)
        counts = jnp.zeros((1, groups), f32)
        for k, block in enumerate(ins[7:]):
            same = gst[pl.ds(me ^ k, 1), :] == mine
            x = block[block.shape[0] - spare :, :].astype(f32)
            sums += jnp.where(same, x[0:1, :groups], 0.0)
            counts += jnp.where(same, x[1:2, :groups], 0.0)
        mean = sums / jnp.maximum(counts, 1.0)
        here = lax.broadcasted_iota(jnp.int32, (groups, groups), 0) == lax.broadcasted_iota(
            jnp.int32, (groups, groups), 1
        )
        mean = jnp.sum(jnp.where(here, mean, 0.0), axis=1, keepdims=True)
        hot = slot[...] == lax.broadcasted_iota(jnp.int32, (groups, n), 0)
        adv = score[...] - jnp.sum(jnp.where(hot, mean, 0.0), axis=0, keepdims=True)
        total = (adv * (t[...] + t_got[...].astype(f32))).astype(bf)
        outs[0][...] = adv
        wide = jnp.concatenate([spread(place[...], total, k) for k in range(groups)], axis=0)
        chunk = width // 2 if width % 256 == 0 else width
        for first in range(0, width, chunk):
            part = jnp.dot(wide, rows[:, first : first + chunk], preferred_element_type=f32)
            part = (scale * part).astype(bf)
            for k in range(groups):
                outs[1 + k][:, first : first + chunk] = part[k * rank : (k + 1) * rank]

    operands = (gst, place, slot_rows, score_rows, t, t_got, rows, *up_blocks)
    out = call(
        kernel,
        [shaped((1, n), f32)] + [shaped((rank, width), bf)] * groups,
        operands,
        [VMEM] * len(operands),
        flops=2 * n * width * rank * groups,
    )
    return out[0], out[1:]


def up_grads(place, adv, t, t_got, cot, groups, after):
    rank, n = t.shape
    cols = cot.shape[1]

    def kernel(ins, outs):
        place, adv, t, t_got, cot = ins
        total = t[...] + t_got[...].astype(f32)
        total = (adv[...] * total).astype(bf)
        wide = jnp.concatenate([spread(place[...], total, k) for k in range(groups)], axis=0)
        part = (scale * jnp.dot(wide, cot[...], preferred_element_type=f32)).astype(bf)
        for k in range(groups):
            outs[k][...] = part[k * rank : (k + 1) * rank]

    return call(
        kernel,
        [shaped((rank, cols), bf)] * groups,
        (place, adv, t, t_got, cot),
        [VMEM] * 5,
        after=after,
        flops=2 * n * cols * rank * groups,
    )


def adapted(place, t, t_got, base_mine, base_got, blocks, after):
    n, cols = base_got.shape
    rank = t.shape[0]

    def kernel(ins, outs):
        place, t, t_got, base_mine, base_got = ins[:5]
        blocks = ins[5:]
        total = (t[...] + t_got[...].astype(f32)).astype(bf)
        wide = jnp.concatenate([spread(place[...], total, k) for k in range(len(blocks))], axis=0)
        ups = jnp.concatenate([up_block(b, rank) for b in blocks], axis=0)
        delta = lax.dot_general(wide, ups, (((0,), (0,)), ((), ())), preferred_element_type=f32)
        delta = (scale * delta).astype(bf).astype(f32)
        outs[0][...] = (base_mine[...].astype(f32) + base_got[...].astype(f32) + delta).astype(bf)

    operands = (place, t, t_got, base_mine, base_got, *blocks)
    return call(
        kernel,
        [shaped((n, cols), bf)],
        operands,
        [VMEM] * len(operands),
        flops=2 * n * cols * rank * len(blocks),
        after=after,
    )[0]


def combine(gst, trp, blocks, filled, after):
    groups = gst.shape[0]
    tasks, rank, width = filled.shape
    count = len(blocks)

    def kernel(*refs):
        tables = refs[:2]
        ins = refs[2 : 2 + count]
        out, held, acc, gst, trp, sem_in, sem_out, sem = refs[-8:]
        loads = [pltpu.make_async_copy(a, b, sem.at[i]) for i, (a, b) in enumerate(zip(tables, (gst, trp)))]
        for c in loads:
            c.start()
        me = lax.axis_index("dp")
        copies = []
        for k in range(groups):
            source = ins[k] if count > 1 else ins[0].at[me ^ k]
            copies.append(pltpu.make_async_copy(source, held.at[k], sem_in.at[k]))
            copies[-1].start()
        for c in loads:
            c.wait()
        rows = [stored_row(gst, trp, tasks, k) for k in range(groups)]
        back = [
            pltpu.make_async_copy(held.at[g], out.at[rows[g]], sem_out.at[g])
            for g in range(groups)
        ]
        last = []
        for g in range(groups):
            ends, again = jnp.bool_(True), jnp.bool_(False)
            for h in range(groups):
                if h > g:
                    ends = jnp.logical_and(ends, rows[h] != rows[g])
                if h < g:
                    again = jnp.logical_or(again, rows[h] == rows[g])
            last.append(ends)
            copies[g].wait()

            @pl.when(jnp.logical_and(ends, again))
            def _():
                acc[...] = held[g].astype(f32)
                for h in range(g):

                    @pl.when(rows[h] == rows[g])
                    def _():
                        acc[...] += held[h].astype(f32)

                held[g] = acc[...].astype(bf)

            @pl.when(ends)
            def _():
                back[g].start()

        for g in range(groups):

            @pl.when(last[g])
            def _():
                back[g].wait()

    return pl.pallas_call(
        kernel,
        out_shape=shaped(filled.shape, bf),
        in_specs=[ANY] * (count + 3 + len(after)),
        out_specs=ANY,
        scratch_shapes=[
            pltpu.VMEM((groups, rank, width), bf),
            pltpu.VMEM((rank, width), f32),
            pltpu.SMEM(gst.shape, jnp.int32),
            pltpu.SMEM(trp.shape, jnp.int32),
            pltpu.SemaphoreType.DMA((groups,)),
            pltpu.SemaphoreType.DMA((groups,)),
            pltpu.SemaphoreType.DMA((2,)),
        ],
        input_output_aliases={2 + count: 0},
        compiler_params=pltpu.CompilerParams(vmem_limit_bytes=big),
        cost_estimate=pl.CostEstimate(flops=0, bytes_accessed=0, transcendentals=0),
    )(gst, trp, *blocks, filled, *after)


def exchange(x):
    return lax.all_to_all(x, "dp", split_axis=0, concat_axis=0, tiled=True)


def partners(blocks):
    got = {k: swap(blocks[k], k, "dp") for k in reversed(range(1, len(blocks)))}
    return [blocks[0]] + [got[k] for k in range(1, len(blocks))]


def body(hidden, weight, down, up, slot, gst, trp, scores, cotangent):
    groups, parts = lax.axis_size("dp"), lax.axis_size("tensor")
    half = groups // 2
    me = lax.axis_index("dp")
    att, steps, width = hidden.shape
    cols = cotangent.shape[2]
    n = att * steps
    tasks, rank = down.shape[0], down.shape[2]
    down = jnp.swapaxes(down, 1, 2)

    slot_row = slot.reshape(1, att)
    score_row = scores.reshape(1, att)
    up_out = pack_up(gst, trp, up, slot_row, score_row)
    up_got = partners(up_out)
    down_out = pack_down(gst, trp, down, (up_out[0],))
    down_got = exchange(lax.optimization_barrier((down_out, *up_got))[0])

    hidden, cotangent, _ = lax.optimization_barrier((hidden, cotangent, up_out[0]))
    cot = cotangent.reshape(n, cols)
    rows = hidden.reshape(n, width)

    back, back_wire, slot_rows, place, score_rows = inner_up(
        slot_row, score_row, cot, up_got, rank, ()
    )
    back, back_got = sum_first(back, back_wire, "tensor")
    adv, down_grad = down_grads(
        gst, place, slot_rows, score_rows, back, back_got, rows, up_got
    )
    late = list(range(half, half + half // 2))
    soon = list(range(half + half // 2, groups))
    down_grad = list(down_grad)
    for k in late:
        down_grad[k] = lax.optimization_barrier((down_grad[k], down_got))[0]
    down_grad_got = partners(down_grad)

    odd, even, zero_down, zero_up = base_parts(
        rows, weight, parts, ((tasks, rank, width), (tasks, rank, cols)), (adv,)
    )
    held, k = [odd, even], 1
    while 2 * k < parts:
        got = swap(held[0], k, "tensor").astype(f32)
        both = (held[1].astype(f32) + got).astype(bf)
        held, k = [both[1::2], both[0::2]], 2 * k
    base_far, base_mine = held[0].reshape(n, cols), held[1].reshape(n, cols)
    base_got = swap(base_far, k, "tensor")

    ahead, ahead_wire = inner_down(slot_rows, rows, down_got, (base_got, *down_grad_got[1:half]))
    ahead, ahead_got = sum_first(ahead, ahead_wire, "tensor")
    kv_new = adapted(place, ahead, ahead_got, base_mine, base_got, up_got, ())
    kv_out = kv_new.reshape(att, steps, cols)
    up_grad = up_grads(
        place, adv, ahead, ahead_got, cot, groups, (kv_out, *[down_grad_got[k] for k in soon])
    )
    up_grad_got = [up_grad[0]] + [None] * (groups - 1)
    for k in [*range(half, groups), *range(1, half)]:
        x = lax.optimization_barrier((up_grad[k], down_grad_got[k]))[0]
        up_grad_got[k] = swap(x, k, "dp")
    grad_down = combine(gst, trp, down_grad_got, zero_down, ())
    grad_up = combine(gst, trp, up_grad_got, zero_up, (grad_down,))
    return (kv_out, jnp.swapaxes(grad_down, 1, 2), grad_up)


def solution(mesh):
    in_specs = (
        P("dp", None, "tensor"),
        P("tensor", None),
        P("dp", "tensor", None),
        P("dp", None, "tensor"),
        P("dp", None),
        P(),
        P(),
        P("dp"),
        P("dp", None, "tensor"),
    )
    out_specs = (P("dp", None, "tensor"), P("dp", "tensor", None), P("dp", None, "tensor"))
    return jax.shard_map(body, mesh=mesh, in_specs=in_specs, out_specs=out_specs, check_vma=False)
```

```python
import functools

import jax
import jax.numpy as jnp
from jax import lax
from jax.experimental import pallas as pl
from jax.experimental.pallas import tpu as pltpu
from jax.sharding import PartitionSpec as P

scale = 0.25
bf = jnp.bfloat16
f32 = jnp.float32
big = 64 * 1024 * 1024
spare = 16
lanes = 128

ANY = pl.BlockSpec(memory_space=pl.ANY)
SMEM = pl.BlockSpec(memory_space=pltpu.SMEM)
VMEM = pl.BlockSpec(memory_space=pltpu.VMEM)


def shaped(shape, dtype):
    return jax.ShapeDtypeStruct(shape, dtype)


def call(kernel, outs, operands, specs, flops=0, scratch=(), after=(), vmem_outs=True):
    moved = sum(a.size * a.dtype.itemsize for a in list(operands) + list(outs))
    count = len(operands)

    def run(*refs):
        kernel(refs[:count], refs[count + len(after) :])

    return pl.pallas_call(
        run,
        out_shape=list(outs),
        in_specs=list(specs) + [ANY] * len(after),
        out_specs=[VMEM] * len(outs),
        scratch_shapes=list(scratch),
        compiler_params=pltpu.CompilerParams(vmem_limit_bytes=big),
        cost_estimate=pl.CostEstimate(flops=0, bytes_accessed=0, transcendentals=0),
    )(*operands, *after)


def swap(x, k, axis):
    n = lax.axis_size(axis)
    return lax.ppermute(x, axis, [(i, i ^ k) for i in range(n)])


def stored_row(gst, trp, tasks, k):
    me = lax.axis_index("dp")
    return lax.rem(trp[gst[me ^ k, me]], tasks)


def pack_up(gst, trp, up, slot_row, score_row):
    groups = gst.shape[0]
    tasks, rank, cols = up.shape
    tiles = cols // lanes

    def kernel(ins, outs):
        gst, trp, up, slot, score = ins
        sem = outs[-1]
        copies = []
        for k in reversed(range(groups)):
            row = stored_row(gst, trp, tasks, k)
            for j in range(tiles):
                copies.append(
                    pltpu.make_async_copy(
                        up.at[row, :, pl.ds(j * lanes, lanes)],
                        outs[k].at[pl.ds(j * rank, rank), :],
                        sem.at[k, j],
                    )
                )
                copies[-1].start()
        hot = slot[...] == lax.broadcasted_iota(jnp.int32, (groups, slot.shape[1]), 0)
        sums = jnp.sum(jnp.where(hot, score[...].astype(f32), 0.0), axis=1, keepdims=True)
        counts = jnp.sum(jnp.where(hot, 1.0, 0.0), axis=1, keepdims=True)
        here = lax.broadcasted_iota(jnp.int32, (groups, lanes), 0) == lax.broadcasted_iota(
            jnp.int32, (groups, lanes), 1
        )
        sums = jnp.sum(jnp.where(here, sums, 0.0), axis=0, keepdims=True)
        counts = jnp.sum(jnp.where(here, counts, 0.0), axis=0, keepdims=True)
        line = lax.broadcasted_iota(jnp.int32, (spare, lanes), 0)
        both = jnp.where(line == 0, sums, jnp.where(line == 1, counts, 0.0)).astype(bf)
        for k in range(groups):
            outs[k][tiles * rank :, :] = both
        for c in copies:
            c.wait()

    return call(
        kernel,
        [shaped((tiles * rank + spare, lanes), bf)] * groups,
        (gst, trp, up, slot_row, score_row),
        [SMEM, SMEM, ANY, VMEM, VMEM],
        scratch=[pltpu.SemaphoreType.DMA((groups, tiles))],
    )


def up_block(block, rank):
    tiles = block.shape[0] // rank
    return jnp.concatenate([block[j * rank : (j + 1) * rank, :] for j in range(tiles)], axis=1)


def pack_down(gst, trp, down, after):
    groups = gst.shape[0]
    tasks, rank, width = down.shape

    def kernel(ins, outs):
        gst, trp, down = ins
        out, sem = outs
        me = lax.axis_index("dp")
        copies = []
        for g in range(groups):
            row = lax.rem(trp[gst[g, me]], tasks)
            copies.append(pltpu.make_async_copy(down.at[row], out.at[g], sem.at[g]))
            copies[-1].start()
        for c in copies:
            c.wait()

    return call(
        kernel,
        [shaped((groups, rank, width), bf)],
        (gst, trp, down),
        [SMEM, SMEM, ANY],
        scratch=[pltpu.SemaphoreType.DMA((groups,))],
        after=after,
    )[0]


def base_parts(rows, weight, parts, shapes, after):
    n, width = rows.shape
    cols = weight.shape[1] // parts
    half = parts // 2
    tasks, rank = shapes[0][:2]
    widest = max(x[2] for x in shapes)
    mine = lax.axis_index("tensor").astype(jnp.int32).reshape(1)

    def shard(i, m):
        return m[0] ^ jnp.where(i < half, 2 * i + 1, 2 * (i - half))

    def kernel(mine, rows, weight, *rest):
        odd, even, *zeros, blank, sem = rest[len(after) :]
        step = pl.program_id(0)
        copies = [
            pltpu.make_async_copy(blank.at[:, pl.ds(0, z.shape[2])], z.at[t], sem.at[i, t])
            for i, z in enumerate(zeros)
            for t in range(tasks)
        ]

        @pl.when(step == 0)
        def _():
            blank[...] = jnp.zeros((rank, widest), bf)
            for c in copies:
                c.start()

        part = jnp.dot(rows[...], weight[...], preferred_element_type=f32).astype(bf)

        @pl.when(step < half)
        def _():
            odd[0] = part

        @pl.when(step >= half)
        def _():
            even[0] = part

        @pl.when(step == parts - 1)
        def _():
            for c in copies:
                c.wait()

    return pl.pallas_call(
        kernel,
        out_shape=[shaped((half, n, cols), bf)] * 2 + [shaped(x, bf) for x in shapes],
        grid_spec=pltpu.PrefetchScalarGridSpec(
            num_scalar_prefetch=1,
            grid=(parts,),
            in_specs=[
                pl.BlockSpec((n, width), lambda i, m: (0, 0)),
                pl.BlockSpec((width, cols), lambda i, m: (0, shard(i, m))),
            ]
            + [ANY] * len(after),
            out_specs=[
                pl.BlockSpec((1, n, cols), lambda i, m: (jnp.minimum(i, half - 1), 0, 0)),
                pl.BlockSpec((1, n, cols), lambda i, m: (jnp.maximum(i - half, 0), 0, 0)),
            ]
            + [ANY] * len(shapes),
            scratch_shapes=[
                pltpu.VMEM((rank, widest), bf),
                pltpu.SemaphoreType.DMA((len(shapes), tasks)),
            ],
        ),
        compiler_params=pltpu.CompilerParams(vmem_limit_bytes=big),
        cost_estimate=pl.CostEstimate(flops=0, bytes_accessed=0, transcendentals=0),
    )(mine, rows, weight, *after)


def inner_up(slot_row, score_row, rows, blocks, rank, after):
    n, cols = rows.shape
    att = slot_row.shape[1]
    steps = n // att

    def kernel(ins, outs):
        slot, score, rows = ins[:3]
        start = steps * lax.broadcasted_iota(jnp.int32, (att, n), 0)
        row = lax.broadcasted_iota(jnp.int32, (att, n), 1)
        own = jnp.logical_and(row >= start, row < start + steps).astype(bf)
        line = lax.broadcasted_iota(jnp.int32, (8, att), 0)
        both = jnp.where(line == 0, slot[...], jnp.where(line == 1, score[...], 0))
        both = jnp.dot(both.astype(f32).astype(bf), own, preferred_element_type=f32)
        slots = both[0:1, :].astype(jnp.int32)
        place = slots ^ lax.axis_index("dp")
        outs[2][...] = slots
        outs[3][...] = place
        outs[4][...] = both[1:2, :]
        wide = lax.dot_general(
            jnp.concatenate([up_block(block, rank) for block in ins[3:]], axis=0),
            rows[...],
            (((1,), (1,)), ((), ())),
            preferred_element_type=f32,
        )
        acc = jnp.zeros((rank, n), f32)
        for k in range(len(blocks)):
            acc = jnp.where(place == k, wide[k * rank : (k + 1) * rank], acc)
        outs[0][...] = acc
        outs[1][...] = acc.astype(bf)

    operands = (slot_row, score_row, rows, *blocks)
    return call(
        kernel,
        [shaped((rank, n), f32), shaped((rank, n), bf)]
        + [shaped((1, n), jnp.int32)] * 2
        + [shaped((1, n), f32)],
        operands,
        [VMEM] * len(operands),
        flops=2 * n * cols * rank * len(blocks),
        after=after,
    )


def inner_down(slot_rows, rows, blocks, after):
    groups, rank, width = blocks.shape
    n = rows.shape[0]

    def kernel(ins, outs):
        slot, rows, blocks = ins
        wide = lax.dot_general(
            blocks[...].reshape(groups * rank, width),
            rows[...],
            (((1,), (1,)), ((), ())),
            preferred_element_type=f32,
        )
        acc = jnp.zeros((rank, n), f32)
        for s in range(groups):
            acc = jnp.where(slot[...] == s, wide[s * rank : (s + 1) * rank], acc)
        outs[0][...] = acc
        outs[1][...] = acc.astype(bf)

    return call(
        kernel,
        [shaped((rank, n), f32), shaped((rank, n), bf)],
        (slot_rows, rows, blocks),
        [VMEM] * 3,
        flops=2 * n * width * rank * groups,
        after=after,
    )


def plus(x, got, after):
    def kernel(ins, outs):
        total = ins[0][...] + ins[1][...].astype(f32)
        outs[0][...] = total
        outs[1][...] = total.astype(bf)

    return call(kernel, [shaped(x.shape, f32), shaped(x.shape, bf)], (x, got), [VMEM] * 2, after=after)


def sum_first(x, wire, axis, after=()):
    k = 1
    while 2 * k < lax.axis_size(axis):
        x, wire = plus(x, swap(wire, k, axis), after)
        k *= 2
    return x, swap(wire, k, axis)


def spread(place, inner_t, k):
    return jnp.where(place == k, inner_t, jnp.zeros((), inner_t.dtype))


def down_grads(gst, place, slot_rows, score_rows, t, t_got, rows, up_blocks):
    groups = len(up_blocks)
    rank, n = t.shape
    width = rows.shape[1]

    def kernel(ins, outs):
        gst, place, slot, score, t, t_got, rows = ins[:7]
        me = lax.axis_index("dp")
        mine = gst[pl.ds(me, 1), :]
        sums = jnp.zeros((1, groups), f32)
        counts = jnp.zeros((1, groups), f32)
        for k, block in enumerate(ins[7:]):
            same = gst[pl.ds(me ^ k, 1), :] == mine
            x = block[block.shape[0] - spare :, :].astype(f32)
            sums += jnp.where(same, x[0:1, :groups], 0.0)
            counts += jnp.where(same, x[1:2, :groups], 0.0)
        mean = sums / jnp.maximum(counts, 1.0)
        here = lax.broadcasted_iota(jnp.int32, (groups, groups), 0) == lax.broadcasted_iota(
            jnp.int32, (groups, groups), 1
        )
        mean = jnp.sum(jnp.where(here, mean, 0.0), axis=1, keepdims=True)
        hot = slot[...] == lax.broadcasted_iota(jnp.int32, (groups, n), 0)
        adv = score[...] - jnp.sum(jnp.where(hot, mean, 0.0), axis=0, keepdims=True)
        total = (adv * (t[...] + t_got[...].astype(f32))).astype(bf)
        outs[0][...] = adv
        wide = jnp.concatenate([spread(place[...], total, k) for k in range(groups)], axis=0)
        chunk = width // 2 if width % 256 == 0 else width
        for first in range(0, width, chunk):
            part = jnp.dot(wide, rows[:, first : first + chunk], preferred_element_type=f32)
            part = (scale * part).astype(bf)
            for k in range(groups):
                outs[1 + k][:, first : first + chunk] = part[k * rank : (k + 1) * rank]

    operands = (gst, place, slot_rows, score_rows, t, t_got, rows, *up_blocks)
    out = call(
        kernel,
        [shaped((1, n), f32)] + [shaped((rank, width), bf)] * groups,
        operands,
        [VMEM] * len(operands),
        flops=2 * n * width * rank * groups,
    )
    return out[0], out[1:]


def up_grads(place, adv, t, t_got, cot, groups, after):
    rank, n = t.shape
    cols = cot.shape[1]

    def kernel(ins, outs):
        place, adv, t, t_got, cot = ins
        total = t[...] + t_got[...].astype(f32)
        total = (adv[...] * total).astype(bf)
        wide = jnp.concatenate([spread(place[...], total, k) for k in range(groups)], axis=0)
        part = (scale * jnp.dot(wide, cot[...], preferred_element_type=f32)).astype(bf)
        for k in range(groups):
            outs[k][...] = part[k * rank : (k + 1) * rank]

    return call(
        kernel,
        [shaped((rank, cols), bf)] * groups,
        (place, adv, t, t_got, cot),
        [VMEM] * 5,
        after=after,
        flops=2 * n * cols * rank * groups,
    )


def adapted(place, t, t_got, base_mine, base_got, blocks, after):
    n, cols = base_got.shape
    rank = t.shape[0]

    def kernel(ins, outs):
        place, t, t_got, base_mine, base_got = ins[:5]
        blocks = ins[5:]
        total = (t[...] + t_got[...].astype(f32)).astype(bf)
        wide = jnp.concatenate([spread(place[...], total, k) for k in range(len(blocks))], axis=0)
        ups = jnp.concatenate([up_block(b, rank) for b in blocks], axis=0)
        delta = lax.dot_general(wide, ups, (((0,), (0,)), ((), ())), preferred_element_type=f32)
        delta = (scale * delta).astype(bf).astype(f32)
        outs[0][...] = (base_mine[...].astype(f32) + base_got[...].astype(f32) + delta).astype(bf)

    operands = (place, t, t_got, base_mine, base_got, *blocks)
    return call(
        kernel,
        [shaped((n, cols), bf)],
        operands,
        [VMEM] * len(operands),
        flops=2 * n * cols * rank * len(blocks),
        after=after,
    )[0]


def combine(gst, trp, blocks, filled, after):
    groups = gst.shape[0]
    tasks, rank, width = filled.shape
    count = len(blocks)

    def kernel(*refs):
        tables = refs[:2]
        ins = refs[2 : 2 + count]
        out, held, acc, gst, trp, sem_in, sem_out, sem = refs[-8:]
        loads = [pltpu.make_async_copy(a, b, sem.at[i]) for i, (a, b) in enumerate(zip(tables, (gst, trp)))]
        for c in loads:
            c.start()
        me = lax.axis_index("dp")
        copies = []
        for k in range(groups):
            source = ins[k] if count > 1 else ins[0].at[me ^ k]
            copies.append(pltpu.make_async_copy(source, held.at[k], sem_in.at[k]))
            copies[-1].start()
        for c in loads:
            c.wait()
        rows = [stored_row(gst, trp, tasks, k) for k in range(groups)]
        back = [
            pltpu.make_async_copy(held.at[g], out.at[rows[g]], sem_out.at[g])
            for g in range(groups)
        ]
        last = []
        for g in range(groups):
            ends, again = jnp.bool_(True), jnp.bool_(False)
            for h in range(groups):
                if h > g:
                    ends = jnp.logical_and(ends, rows[h] != rows[g])
                if h < g:
                    again = jnp.logical_or(again, rows[h] == rows[g])
            last.append(ends)
            copies[g].wait()

            @pl.when(jnp.logical_and(ends, again))
            def _():
                acc[...] = held[g].astype(f32)
                for h in range(g):

                    @pl.when(rows[h] == rows[g])
                    def _():
                        acc[...] += held[h].astype(f32)

                held[g] = acc[...].astype(bf)

            @pl.when(ends)
            def _():
                back[g].start()

        for g in range(groups):

            @pl.when(last[g])
            def _():
                back[g].wait()

    return pl.pallas_call(
        kernel,
        out_shape=shaped(filled.shape, bf),
        in_specs=[ANY] * (count + 3 + len(after)),
        out_specs=ANY,
        scratch_shapes=[
            pltpu.VMEM((groups, rank, width), bf),
            pltpu.VMEM((rank, width), f32),
            pltpu.SMEM(gst.shape, jnp.int32),
            pltpu.SMEM(trp.shape, jnp.int32),
            pltpu.SemaphoreType.DMA((groups,)),
            pltpu.SemaphoreType.DMA((groups,)),
            pltpu.SemaphoreType.DMA((2,)),
        ],
        input_output_aliases={2 + count: 0},
        compiler_params=pltpu.CompilerParams(vmem_limit_bytes=big),
        cost_estimate=pl.CostEstimate(flops=0, bytes_accessed=0, transcendentals=0),
    )(gst, trp, *blocks, filled, *after)


def exchange(x):
    return lax.all_to_all(x, "dp", split_axis=0, concat_axis=0, tiled=True)


def partners(blocks):
    got = {k: swap(blocks[k], k, "dp") for k in reversed(range(1, len(blocks)))}
    return [blocks[0]] + [got[k] for k in range(1, len(blocks))]


def body(hidden, weight, down, up, slot, gst, trp, scores, cotangent):
    groups, parts = lax.axis_size("dp"), lax.axis_size("tensor")
    half = groups // 2
    me = lax.axis_index("dp")
    att, steps, width = hidden.shape
    cols = cotangent.shape[2]
    n = att * steps
    tasks, rank = down.shape[0], down.shape[2]
    down = jnp.swapaxes(down, 1, 2)

    slot_row = slot.reshape(1, att)
    score_row = scores.reshape(1, att)
    up_out = pack_up(gst, trp, up, slot_row, score_row)
    up_got = partners(up_out)
    down_out = pack_down(gst, trp, down, (up_out[0],))
    down_got = exchange(lax.optimization_barrier((down_out, *up_got))[0])

    hidden, cotangent, _ = lax.optimization_barrier((hidden, cotangent, up_out[0]))
    cot = cotangent.reshape(n, cols)
    rows = hidden.reshape(n, width)

    back, back_wire, slot_rows, place, score_rows = inner_up(
        slot_row, score_row, cot, up_got, rank, ()
    )
    back, back_got = sum_first(back, back_wire, "tensor")
    adv, down_grad = down_grads(
        gst, place, slot_rows, score_rows, back, back_got, rows, up_got
    )
    late = list(range(half, half + half // 2))
    soon = list(range(half + half // 2, groups))
    down_grad = list(down_grad)
    for k in late:
        down_grad[k] = lax.optimization_barrier((down_grad[k], down_got))[0]
    down_grad_got = partners(down_grad)

    odd, even, zero_down, zero_up = base_parts(
        rows, weight, parts, ((tasks, rank, width), (tasks, rank, cols)), (adv,)
    )
    held, k = [odd, even], 1
    while 2 * k < parts:
        got = swap(held[0], k, "tensor").astype(f32)
        both = (held[1].astype(f32) + got).astype(bf)
        held, k = [both[1::2], both[0::2]], 2 * k
    base_far, base_mine = held[0].reshape(n, cols), held[1].reshape(n, cols)
    base_got = swap(base_far, k, "tensor")

    ahead, ahead_wire = inner_down(slot_rows, rows, down_got, (base_got, *down_grad_got[1:half]))
    ahead, ahead_got = sum_first(ahead, ahead_wire, "tensor")
    kv_new = adapted(place, ahead, ahead_got, base_mine, base_got, up_got, ())
    kv_out = kv_new.reshape(att, steps, cols)
    up_grad = up_grads(
        place, adv, ahead, ahead_got, cot, groups, (kv_out, down_grad_got[soon[-1]])
    )
    up_grad_got = [up_grad[0]] + [None] * (groups - 1)
    for k in [*range(half, groups), *range(1, half)]:
        x = lax.optimization_barrier((up_grad[k], down_grad_got[k]))[0]
        up_grad_got[k] = swap(x, k, "dp")
    grad_down = combine(gst, trp, down_grad_got, zero_down, ())
    grad_up = combine(gst, trp, up_grad_got, zero_up, (grad_down,))
    return (kv_out, jnp.swapaxes(grad_down, 1, 2), grad_up)


def solution(mesh):
    in_specs = (
        P("dp", None, "tensor"),
        P("tensor", None),
        P("dp", "tensor", None),
        P("dp", None, "tensor"),
        P("dp", None),
        P(),
        P(),
        P("dp"),
        P("dp", None, "tensor"),
    )
    out_specs = (P("dp", None, "tensor"), P("dp", "tensor", None), P("dp", None, "tensor"))
    return jax.shard_map(body, mesh=mesh, in_specs=in_specs, out_specs=out_specs, check_vma=False)
```
